256 devices in a mesh: ctx: 32 (over x, y, core), head: 8 (over z).
Axes of the slice: x: 4, y: 4, z: 8, core: 2. Of those that a mesh axis runs over, the one named last changes fastest.
Arguments:
- queries: bfloat16 [4, 32, 8192], P(None, 'ctx', 'head')
- kv_cache: bfloat16 [32, 256, 2, 64, 1024], P(None, 'ctx', None, None, 'head'), may hold values from -6 to 6
- new_kv: bfloat16 [4, 32, 2, 1024], P(None, 'ctx', None, 'head'), may hold values from -6 to 6
- selected: int32 [4, 32, 8, 20], P(None, None, 'head'), may hold values from 0 to 255, as said below
- out_weight: bfloat16 [8192, 8192], P('head', 'ctx'), may hold values from -0.0625 to 0.0625
Outputs:
- mixed: bfloat16 [32, 4, 8192], P('head', None, 'ctx')
The draws below stay inside these ranges and needn't reach their ends.
Inputs may be any that keep to these rules, and one draw needn't show every extreme that they name: Each list selected[s, b, k] names 20 distinct pages; at most 4 of them lie in one aligned block of pages 8 * i to 8 * i + 8 - 1 (the pages of one index of ctx), and exactly 4 in some such block of every list.
All inputs are finite; a program needn't handle non-finite values.
Results may differ from the reference program's by a relative error of at most 0.022.
Values may be sent and summed in bfloat16 or wider, within the bound.
A program may use at most 128 MiB of HBM per device.

```python
import jax
import jax.numpy as jnp
from jax import lax

HQ = 64
KVH = 8
HD = 128
D = 8192
PAGE = 64
S = 4
P_DEV = 8
CAP = 4
BATCH = 32
PAGES = 256
SEL = 20
N_CTX = 32


def draw_queries(key, part):
    key = jax.random.fold_in(key, 1)
    key_base = jax.random.fold_in(key, 0)
    base = jax.random.normal(key_base, (S, BATCH, HQ * HD), jnp.float32)
    base = jnp.clip(base, -6.0, 6.0)
    return base.astype(jnp.bfloat16)


def draw_selected(key, part):
    key = jax.random.fold_in(key, 2)
    keys = jax.random.split(key, S * BATCH * KVH)

    def one_list(single):
        key_a, key_b, key_c, key_d, key_e = jax.random.split(single, 5)
        hottest = jax.random.randint(key_a, (), 0, N_CTX)
        hot_pages = hottest * P_DEV + jax.random.permutation(key_b, P_DEV)[:CAP]
        others = jax.random.permutation(key_c, N_CTX - 1)[:N_CTX // 2]
        others = jnp.where(others >= hottest, others + 1, others)
        spread = others * P_DEV + jax.random.randint(key_d, (N_CTX // 2,), 0, P_DEV)
        listed = jnp.concatenate([hot_pages, spread]).astype(jnp.int32)
        return jnp.take(listed, jax.random.permutation(key_e, SEL))
    return jax.vmap(one_list)(keys).reshape(S, BATCH, KVH, SEL).astype(jnp.int32)


def block_scale(own_key, shape, shards, smallest, top_value):
    loudness = 1.0
    for position, parts in shards:
        draws = jax.random.uniform(jax.random.fold_in(jax.random.fold_in(own_key, 6), position), (parts,), jnp.float32, smallest / len(shards), top_value / len(shards))
        loudness = loudness * jnp.repeat(jnp.exp(draws), shape[position] // parts).reshape((-1,) + (1,) * (len(shape) - 1 - position))
    return loudness


def centred(stream_key, dims, scale, bound, cuts=(), held_as=jnp.bfloat16):
    drawn = jax.random.normal(stream_key, dims, jnp.float32) * scale
    if len(cuts) > 0:
        drawn = block_scale(stream_key, dims, cuts, -0.22, 0.18) * drawn
    return jnp.clip(drawn, min=-bound, max=bound).astype(held_as)


def setup_inputs(seed: int = 0) -> dict:
    arg_keys = jax.random.split(jax.random.key(seed), 6)
    return {
        "queries": draw_queries(jax.random.fold_in(arg_keys[5], 71), 0),
        "kv_cache": centred(arg_keys[1], (BATCH, PAGES, 2, PAGE, KVH * HD), 1.0, 6.0, ((1, 32), (4, 8))),
        "new_kv": centred(arg_keys[2], (S, BATCH, 2, KVH * HD), 1.0, 6.0, ((1, 32), (3, 8))),
        "selected": draw_selected(jax.random.fold_in(arg_keys[5], 71), 0),
        "out_weight": centred(arg_keys[4], (HQ * HD, D), (HQ * HD) ** -0.5, 0.0625, ((0, 8), (1, 32))),
    }


NEG = -1.0e30


def reference(queries, kv_cache, new_kv, selected, out_weight):
    steps = queries.shape[0]
    batch = queries.shape[1]
    groups = HQ // KVH
    scale = HD ** -0.5
    q_all = queries.reshape(steps, batch, KVH, groups, HD)
    cache = kv_cache.reshape(batch, PAGES, 2, PAGE, KVH, HD)
    new_all = new_kv.reshape(steps, batch, 2, KVH, HD)
    causal = jnp.arange(steps)[None, :] <= jnp.arange(steps)[:, None]

    def one_head(cache_head, chosen, q_head, new_head):
        got = cache_head[chosen]
        keys = got[:, :, 0].reshape(steps, SEL * PAGE, HD).astype(jnp.float32)
        vals = got[:, :, 1].reshape(steps, SEL * PAGE, HD).astype(jnp.float32)
        q_float = q_head.astype(jnp.float32)
        new_float = new_head.astype(jnp.float32)
        old_scores = jnp.einsum('sgd,std->sgt', q_float, keys) * scale
        new_scores = jnp.einsum('sgd,rd->sgr', q_float, new_float[:, 0]) * scale
        new_scores = jnp.where(causal[:, None, :], new_scores, NEG)
        scores = jnp.concatenate([old_scores, new_scores], axis=-1)
        top_score = jnp.max(scores, axis=-1, keepdims=True)
        expo = jnp.exp(scores - top_score)
        total = jnp.sum(expo, axis=-1)
        rounded = expo.astype(jnp.bfloat16).astype(jnp.float32)
        weighted = jnp.einsum('sgt,std->sgd', rounded[..., :SEL * PAGE], vals)
        weighted = weighted + jnp.einsum('sgr,rd->sgd', rounded[..., SEL * PAGE:], new_float[:, 1])
        return weighted / total[..., None]

    def one_seq(index):
        cache_seq = jnp.moveaxis(cache[index], 3, 0)
        chosen = jnp.moveaxis(selected[:, index], 1, 0)
        q_seq = jnp.moveaxis(q_all[:, index], 1, 0)
        new_seq = jnp.moveaxis(new_all[:, index], 2, 0)
        result = jax.vmap(one_head)(cache_seq, chosen, q_seq, new_seq)
        return jnp.moveaxis(result, 0, 1).reshape(steps, HQ * HD).astype(jnp.bfloat16)

    attention = lax.map(one_seq, jnp.arange(batch))
    mixed = jnp.einsum('bsf,fd->bsd', attention.astype(jnp.float32), out_weight.astype(jnp.float32))
    return mixed.astype(jnp.bfloat16)
```

```python
import functools
import math

import jax
import jax.numpy as jnp
from jax import lax
from jax.experimental import pallas as pl
from jax.experimental.pallas import tpu as pltpu
from jax.sharding import PartitionSpec as P

HQ = 64
KVH = 8
HD = 128
PAGE = 64
GROUPS = HQ // KVH

NEG = -1e30
EXPONENT = HD ** (-0.5) * math.log2(math.e)
BF16 = jnp.bfloat16
F32 = jnp.float32
MESH = pl.DeviceIdType.MESH


def grid_of(size):
    return {32: (4, 4, 2), 8: (2, 2, 2), 4: (2, 1, 2)}[size]


def shifted(me, k, size):
    nx, ny, nc = grid_of(size)
    x, y, c = me // (ny * nc), (me // nc) % ny, me % nc
    dx, dy, dc = k // (ny * nc), (k // nc) % ny, k % nc
    return (((x + dx) % nx) * ny + (y + dy) % ny) * nc + (c + dc) % nc


def softmax_part(scores, values):
    top = jnp.max(scores, axis=-1, keepdims=True)
    expo = jnp.exp2((scores - top) * EXPONENT)
    total = jnp.sum(expo, axis=-1, keepdims=True)
    weighted = jnp.dot(expo.astype(BF16), values, preferred_element_type=F32)
    return weighted * (1.0 / total), top * EXPONENT + jnp.log2(total)


def packed(normed, logs):
    lane = lax.broadcasted_iota(jnp.int32, (8, HD), 1)
    stats = jnp.zeros((8, HD), F32)
    for v in range(normed.shape[0] // 8):
        stats = jnp.where(lane == v, logs[8 * v : 8 * v + 8], stats)
    high = stats.astype(BF16).astype(F32)
    return jnp.concatenate([normed, high, stats - high], axis=0).astype(BF16)


def kernel(
    q_hbm,
    kv_hbm,
    new_hbm,
    sel_hbm,
    w_hbm,
    out_ref,
    q_in,
    new_in,
    sel_in,
    kv,
    w,
    rows32,
    q_all,
    bias,
    part_out,
    part_in,
    att_all,
    att32,
    mix_out,
    mix_in,
    small_sem,
    kv_sem,
    w_sem,
    q_send,
    q_recv,
    part_send,
    part_recv,
    att_send,
    att_recv,
    mix_send,
    mix_recv,
    *,
    n_ctx,
    n_head,
    group,
):
    steps = q_in.shape[0]
    pages = kv.shape[1]
    tokens = pages * PAGE
    rows = steps * GROUPS
    me = lax.axis_index("ctx")
    my_head = lax.axis_index("head")

    def owner(k):
        return shifted(me, k, n_ctx)

    q_copy = pltpu.make_async_copy(q_hbm, q_in, small_sem.at[0])
    sel_copy = pltpu.make_async_copy(sel_hbm, sel_in, small_sem.at[1])
    new_copy = pltpu.make_async_copy(new_hbm, new_in, small_sem.at[2])
    w_copy = pltpu.make_async_copy(w_hbm, w, w_sem)
    q_copy.start()
    sel_copy.start()
    new_copy.start()

    barrier = pltpu.get_barrier_semaphore()

    @pl.loop(1, n_ctx)
    def _(k):
        pl.semaphore_signal(barrier, inc=1, device_id={"ctx": owner(k)}, device_id_type=MESH)

    @pl.loop(1, n_head)
    def _(k):
        pl.semaphore_signal(
            barrier, inc=1, device_id={"head": (my_head + k) % n_head}, device_id_type=MESH
        )

    def kv_copy(k):
        b = owner(k)
        return pltpu.make_async_copy(kv_hbm.at[b], kv.at[b], kv_sem.at[k])

    @pl.loop(0, n_ctx)
    def _(k):
        kv_copy(k).start()

    w_copy.start()

    q_copy.wait()
    for g in range(GROUPS):
        rows32[g * steps : (g + 1) * steps, :] = q_in[:, g * HD : (g + 1) * HD].astype(F32)
    q_all[me] = rows32[...].astype(BF16)

    pl.semaphore_wait(barrier, n_ctx - 1 + n_head - 1)

    @pl.loop(1, n_ctx)
    def _(k):
        pltpu.make_async_remote_copy(
            src_ref=q_all.at[me],
            dst_ref=q_all.at[me],
            send_sem=q_send,
            recv_sem=q_recv.at[me],
            device_id={"ctx": owner(k)},
            device_id_type=MESH,
        ).start()

    sel_copy.wait()
    number = lax.broadcasted_iota(jnp.int32, (pages, n_ctx), 0) + me * pages
    from_b = lax.broadcasted_iota(jnp.int32, (n_ctx, n_ctx * 8), 0)
    to_lane = lax.broadcasted_iota(jnp.int32, (n_ctx, n_ctx * 8), 1)
    chosen = jnp.zeros((pages, n_ctx * 8), F32)
    for s in range(steps):
        hit = jnp.zeros((pages, n_ctx), F32)
        for j in range(sel_in.shape[1]):
            hit = jnp.where(sel_in[s, j] == number, 1.0, hit)
        spread = jnp.where(((to_lane >> 3) == from_b) & ((to_lane & 3) == s), 1.0, 0.0)
        chosen += jnp.dot(hit.astype(BF16), spread.astype(BF16), preferred_element_type=F32)
    page = lax.broadcasted_iota(jnp.int32, (pages, tokens), 0)
    token = lax.broadcasted_iota(jnp.int32, (pages, tokens), 1)
    expand = jnp.where((token >> 6) == page, 1.0, 0.0).astype(BF16)
    count = lax.dot_general(
        chosen.astype(BF16), expand, (((0,), (0,)), ((), ())), preferred_element_type=F32
    )
    bias[...] = ((count - 1.0) * -NEG).reshape(bias.shape)

    new_copy.wait()
    new_keys = jnp.concatenate(
        [new_in[:, 0].astype(F32), jnp.zeros((HD - steps, HD), F32)], axis=0
    ).astype(BF16)
    new_values = jnp.concatenate(
        [new_in[:, 1].astype(F32), jnp.zeros((HD - steps, HD), F32)], axis=0
    ).astype(BF16)
    fresh = lax.dot_general(
        q_all[me], new_keys, (((1,), (1,)), ((), ())), preferred_element_type=F32
    )
    step_of = lax.broadcasted_iota(jnp.int32, (rows, HD), 0) & (steps - 1)
    place = lax.broadcasted_iota(jnp.int32, (rows, HD), 1)
    fresh = jnp.where(place <= step_of, fresh, NEG)
    part_in[n_ctx] = packed(*softmax_part(fresh, new_values))

    @pl.loop(0, n_ctx // group)
    def _(turn):
        for u in range(group):
            k = turn * group + u
            kv_copy(k).wait()

            def wait_query():
                b = owner(k)
                pltpu.make_async_copy(q_all.at[b], q_all.at[b], q_recv.at[b]).wait()

            if u == 0:
                pl.when(turn > 0)(wait_query)
            else:
                wait_query()
        results = []
        for u in range(group):
            b = owner(turn * group + u)
            keys = kv[b, :, 0].reshape(tokens, HD)
            scores = lax.dot_general(
                q_all[b], keys, (((1,), (1,)), ((), ())), preferred_element_type=F32
            )
            scores = (scores.reshape(rows // 8, 8, tokens) + bias[b][None]).reshape(rows, tokens)
            values = kv[b, :, 1].reshape(tokens, HD)
            results.append(packed(*softmax_part(scores, values)))
        for u in range(group):
            part_out[turn * group + u] = results[u]
        for u in range(group):
            k = turn * group + u

            def send():
                pltpu.make_async_remote_copy(
                    src_ref=part_out.at[k],
                    dst_ref=part_in.at[me],
                    send_sem=part_send,
                    recv_sem=part_recv,
                    device_id={"ctx": owner(k)},
                    device_id_type=MESH,
                ).start()

            if u == 0:
                pl.when(turn > 0)(send)
            else:
                send()

    part_in[me] = part_out[0]

    others = pl.ds(0, n_ctx - 1)
    pltpu.make_async_copy(part_in.at[others], part_in.at[others], part_recv).wait()
    logs = [part_in[i, rows : rows + 16, :].astype(F32) for i in range(n_ctx + 1)]
    logs = [pair[0:8] + pair[8:16] for pair in logs]
    top = functools.reduce(jnp.maximum, logs)
    shares = [jnp.exp2(log - top) for log in logs]
    total = functools.reduce(jnp.add, shares)
    inverse = 1.0 / total
    joined = [jnp.zeros((8, HD), F32) for _ in range(rows // 8)]
    for i in range(n_ctx + 1):
        share = shares[i] * inverse
        part = part_in[i, 0:rows, :].astype(F32)
        for v in range(rows // 8):
            joined[v] += part[8 * v : 8 * v + 8] * share[:, v : v + 1]
    rows32[...] = jnp.concatenate(joined, axis=0)
    attention = jnp.concatenate(
        [rows32[pl.ds(s, GROUPS, stride=steps), :] for s in range(steps)], axis=0
    )
    att_all[me] = attention.astype(BF16)

    @pl.loop(1, n_ctx)
    def _(k):
        pltpu.make_async_remote_copy(
            src_ref=att_all.at[me],
            dst_ref=att_all.at[me],
            send_sem=att_send,
            recv_sem=att_recv,
            device_id={"ctx": owner(k)},
            device_id_type=MESH,
        ).start()

    w_copy.wait()
    pltpu.make_async_copy(att_all.at[others], att_all.at[others], att_recv).wait()

    att32[...] = att_all[...].astype(F32).reshape(att32.shape)
    flat = jnp.concatenate(
        [att32[pl.ds(g, n_ctx * steps, stride=GROUPS), :].astype(BF16) for g in range(GROUPS)],
        axis=1,
    )
    mixed = jnp.dot(flat, w[...], preferred_element_type=F32)
    mix_out[...] = mixed.astype(BF16).reshape(mix_out.shape)

    @pl.loop(1, n_head)
    def _(k):
        to = (my_head + k) % n_head
        pltpu.make_async_remote_copy(
            src_ref=mix_out.at[to],
            dst_ref=mix_in.at[my_head],
            send_sem=mix_send,
            recv_sem=mix_recv,
            device_id={"head": to},
            device_id_type=MESH,
        ).start()

    mix_in[my_head] = mix_out[my_head]
    other_heads = pl.ds(0, n_head - 1)
    pltpu.make_async_copy(mix_in.at[other_heads], mix_in.at[other_heads], mix_recv).wait()
    out_ref[...] = jnp.sum(mix_in[...].astype(F32), axis=0).astype(BF16)

    pltpu.make_async_copy(q_all.at[others], q_all.at[others], q_send).wait()
    pltpu.make_async_copy(part_out.at[others], part_out.at[others], part_send).wait()
    pltpu.make_async_copy(att_all.at[others], att_all.at[others], att_send).wait()
    pltpu.make_async_copy(mix_out.at[other_heads], mix_out.at[other_heads], mix_send).wait()


def local(queries, kv_cache, new_kv, selected, out_weight, *, n_ctx, n_head, group):
    steps, _, width = queries.shape
    batch, pages = kv_cache.shape[:2]
    rows = steps * GROUPS
    columns = out_weight.shape[1]
    own = batch // n_head * steps
    dma = pltpu.SemaphoreType.DMA
    any_space = pl.BlockSpec(memory_space=pl.ANY)
    sel = jnp.transpose(selected, (0, 3, 2, 1))
    result = pl.pallas_call(
        functools.partial(kernel, n_ctx=n_ctx, n_head=n_head, group=group),
        out_shape=jax.ShapeDtypeStruct((own, columns), BF16),
        in_specs=[any_space] * 5,
        out_specs=pl.BlockSpec(memory_space=pltpu.VMEM),
        scratch_shapes=[
            pltpu.VMEM((steps, width), BF16),
            pltpu.VMEM((steps, 2, HD), BF16),
            pltpu.VMEM(sel.shape, jnp.int32),
            pltpu.VMEM(kv_cache.shape, BF16),
            pltpu.VMEM(out_weight.shape, BF16),
            pltpu.VMEM((rows, HD), F32),
            pltpu.VMEM((batch, rows, HD), BF16),
            pltpu.VMEM((batch, 8, pages * PAGE), F32),
            pltpu.VMEM((n_ctx, rows + 16, HD), BF16),
            pltpu.VMEM((n_ctx + 1, rows + 16, HD), BF16),
            pltpu.VMEM((batch, rows, HD), BF16),
            pltpu.VMEM((batch * rows, HD), F32),
            pltpu.VMEM((n_head, own, columns), BF16),
            pltpu.VMEM((n_head, own, columns), BF16),
            dma((3,)),
            dma((n_ctx,)),
            dma,
            dma,
            dma((n_ctx,)),
            dma,
            dma,
            dma,
            dma,
            dma,
            dma,
        ],
        compiler_params=pltpu.CompilerParams(
            collective_id=0, has_side_effects=True, vmem_limit_bytes=56 * 1024 * 1024
        ),
    )(
        queries.reshape(steps, width),
        kv_cache,
        new_kv.reshape(steps, 2, HD),
        sel,
        out_weight,
    )
    return result.reshape(batch // n_head, steps, columns)


def solution(mesh):
    n_ctx, n_head = mesh.shape["ctx"], mesh.shape["head"]
    return jax.shard_map(
        functools.partial(local, n_ctx=n_ctx, n_head=n_head, group=4),
        mesh=mesh,
        in_specs=(
            P(None, "ctx", "head"),
            P(None, "ctx", None, None, "head"),
            P(None, "ctx", None, "head"),
            P(None, None, "head", None),
            P("head", "ctx"),
        ),
        out_specs=P("head", None, "ctx"),
        check_vma=False,
    )
```

```python
import functools
import math

import jax
import jax.numpy as jnp
from jax import lax
from jax.experimental import pallas as pl
from jax.experimental.pallas import tpu as pltpu
from jax.sharding import PartitionSpec as P

HQ = 64
KVH = 8
HD = 128
PAGE = 64
GROUPS = HQ // KVH

NEG = -1e30
EXPONENT = HD ** (-0.5) * math.log2(math.e)
BF16 = jnp.bfloat16
F32 = jnp.float32
MESH = pl.DeviceIdType.MESH


def displacements(size):
    sizes = {32: (4, 4, 2), 8: (2, 2, 2), 4: (2, 1, 2)}[size]
    nx, ny, nc = sizes
    every = [(x, y, c) for x in range(nx) for y in range(ny) for c in range(nc)][1:]

    def hops(d):
        return min(d[0], nx - d[0]) + min(d[1], ny - d[1])

    every = sorted(every, key=lambda d: -hops(d))
    parts = [[d for d in every if hops(d) >= 3], [d for d in every if hops(d) == 2], [d for d in every if hops(d) < 2]]
    return sizes, [part for part in parts if part]


def by_distance(size):
    return sorted(range(1, size), key=lambda d: -min(d, size - d))


def softmax_parts(queries, keys, values, masked):
    scores = [
        mask(lax.dot_general(q, k, (((1,), (1,)), ((), ())), preferred_element_type=F32))
        for q, k, mask in zip(queries, keys, masked)
    ]
    tops = [jnp.max(x, axis=-1, keepdims=True) for x in scores]
    expos = [jnp.exp2((x - top) * EXPONENT) for x, top in zip(scores, tops)]
    totals = [jnp.sum(x, axis=-1, keepdims=True) for x in expos]
    sums = [
        jnp.dot(x.astype(BF16), v, preferred_element_type=F32) for x, v in zip(expos, values)
    ]
    return [
        ((x * (1.0 / total)).astype(BF16), as_row(top * EXPONENT + jnp.log2(total)))
        for x, top, total in zip(sums, tops, totals)
    ]


def as_row(column):
    lane = lax.broadcasted_iota(jnp.int32, (8, HD), 1)
    sublane = lax.broadcasted_iota(jnp.int32, (8, HD), 0)
    spread = jnp.zeros((8, HD), F32)
    for v in range(column.shape[0] // 8):
        spread = jnp.where(lane == sublane + 8 * v, column[8 * v : 8 * v + 8], spread)
    return jnp.sum(spread, axis=0, keepdims=True)


def kernel(
    q_hbm,
    kv_hbm,
    new_hbm,
    sel_hbm,
    w_hbm,
    out_ref,
    q_in,
    new_in,
    sel_in,
    kv,
    w,
    rows32,
    q_all,
    bias,
    part_out,
    part_in,
    log_out,
    log_in,
    att_all,
    att32,
    mix_out,
    mix_in,
    small_sem,
    kv_sem,
    w_sem,
    q_send,
    q_recv,
    part_send,
    part_recv,
    log_send,
    log_recv,
    att_send,
    att_recv,
    mix_send,
    mix_recv,
    *,
    n_ctx,
    n_head,
):
    steps = q_in.shape[0]
    pages = kv.shape[1]
    tokens = pages * PAGE
    rows = steps * GROUPS
    me = lax.axis_index("ctx")
    my_head = lax.axis_index("head")

    (nx, ny, nc), parts = displacements(n_ctx)
    others_list = [d for part in parts for d in part]
    x, y, c = me // (ny * nc), (me // nc) & (ny - 1), me & (nc - 1)

    def owner(d):
        return (((x + d[0]) & (nx - 1)) * ny + ((y + d[1]) & (ny - 1))) * nc + ((c + d[2]) & (nc - 1))

    def back(d):
        opposite = ((nx - d[0]) % nx, (ny - d[1]) % ny, (nc - d[2]) % nc)
        return next(i for i, part in enumerate(parts) if opposite in part)

    q_copy = pltpu.make_async_copy(q_hbm, q_in, small_sem.at[0])
    sel_copy = pltpu.make_async_copy(sel_hbm, sel_in, small_sem.at[1])
    new_copy = pltpu.make_async_copy(new_hbm, new_in, small_sem.at[2])
    w_copy = pltpu.make_async_copy(w_hbm, w, w_sem)
    q_copy.start()
    sel_copy.start()
    new_copy.start()

    barrier = pltpu.get_barrier_semaphore()

    for d in others_list:
        pl.semaphore_signal(barrier, inc=1, device_id={"ctx": owner(d)}, device_id_type=MESH)
    for d in by_distance(n_head):
        to = lax.rem(my_head + d, n_head)
        pl.semaphore_signal(barrier, inc=1, device_id={"head": to}, device_id_type=MESH)

    chunk = kv.shape[0] // 4
    for i in range(4):
        part = pl.ds(i * chunk, chunk)
        pltpu.make_async_copy(kv_hbm.at[part], kv.at[part], kv_sem).start()
    w_copy.start()

    q_copy.wait()
    for g in range(GROUPS):
        rows32[g * steps : (g + 1) * steps, :] = q_in[:, g * HD : (g + 1) * HD].astype(F32)
    q_all[me] = rows32[...].astype(BF16)

    pl.semaphore_wait(barrier, n_ctx - 1 + n_head - 1)

    for d in others_list:
        pltpu.make_async_remote_copy(
            src_ref=q_all.at[me],
            dst_ref=q_all.at[me],
            send_sem=q_send,
            recv_sem=q_recv.at[back(d)],
            device_id={"ctx": owner(d)},
            device_id_type=MESH,
        ).start()

    sel_copy.wait()
    number = lax.broadcasted_iota(jnp.int32, (pages, n_ctx), 0) + me * pages
    from_b = lax.broadcasted_iota(jnp.int32, (n_ctx, n_ctx * 8), 0)
    to_lane = lax.broadcasted_iota(jnp.int32, (n_ctx, n_ctx * 8), 1)
    chosen = jnp.zeros((pages, n_ctx * 8), F32)
    for s in range(steps):
        hit = jnp.zeros((pages, n_ctx), F32)
        for j in range(sel_in.shape[1]):
            hit = jnp.where(sel_in[s, j] == number, 1.0, hit)
        spread = jnp.where(((to_lane >> 3) == from_b) & ((to_lane & 3) == s), 1.0, 0.0)
        chosen += jnp.dot(hit.astype(BF16), spread.astype(BF16), preferred_element_type=F32)
    page = lax.broadcasted_iota(jnp.int32, (pages, tokens), 0)
    token = lax.broadcasted_iota(jnp.int32, (pages, tokens), 1)
    expand = jnp.where((token >> 6) == page, 1.0, 0.0).astype(BF16)
    count = lax.dot_general(
        chosen.astype(BF16), expand, (((0,), (0,)), ((), ())), preferred_element_type=F32
    )
    bias[...] = ((count - 1.0) * -NEG).reshape(bias.shape)

    new_copy.wait()
    new_keys = jnp.concatenate(
        [new_in[:, 0].astype(F32), jnp.zeros((HD - steps, HD), F32)], axis=0
    ).astype(BF16)
    new_values = jnp.concatenate(
        [new_in[:, 1].astype(F32), jnp.zeros((HD - steps, HD), F32)], axis=0
    ).astype(BF16)
    step_of = lax.broadcasted_iota(jnp.int32, (rows, HD), 0) & (steps - 1)
    place = lax.broadcasted_iota(jnp.int32, (rows, HD), 1)

    def causal(scores):
        return jnp.where(place <= step_of, scores, NEG)

    def selected_of(b):
        def mask(scores):
            return (scores.reshape(rows // 8, 8, tokens) + bias[b][None]).reshape(rows, tokens)

        return mask

    def keys_of(b):
        return kv[b, :, 0].reshape(tokens, HD)

    def values_of(b):
        return kv[b, :, 1].reshape(tokens, HD)

    pltpu.make_async_copy(kv, kv, kv_sem).wait()
    own = q_all[me]
    (fresh_part, fresh_log), (own_part, own_log) = softmax_parts(
        [own, own], [new_keys, keys_of(me)], [new_values, values_of(me)], [causal, selected_of(me)]
    )
    part_in[n_ctx], log_in[n_ctx] = fresh_part, fresh_log
    part_in[me], log_in[me] = own_part, own_log
    for i in range(n_ctx + 1, log_in.shape[0]):
        log_in[i] = jnp.full((1, HD), NEG, F32)

    done = 0
    for i, part in enumerate(parts):
        block = pl.ds(0, len(part))
        pltpu.make_async_copy(q_all.at[block], q_all.at[block], q_recv.at[i]).wait()
        owners = [owner(d) for d in part]
        results = softmax_parts(
            [q_all[b] for b in owners],
            [keys_of(b) for b in owners],
            [values_of(b) for b in owners],
            [selected_of(b) for b in owners],
        )
        for u, (normed, log) in enumerate(results):
            part_out[done + u], log_out[done + u] = normed, log
        for u, b in enumerate(owners):
            for out, into, send_sem, recv_sem in (
                (log_out, log_in, log_send, log_recv),
                (part_out, part_in, part_send, part_recv),
            ):
                pltpu.make_async_remote_copy(
                    src_ref=out.at[done + u],
                    dst_ref=into.at[me],
                    send_sem=send_sem,
                    recv_sem=recv_sem,
                    device_id={"ctx": b},
                    device_id_type=MESH,
                ).start()
        done += len(part)

    others = pl.ds(0, n_ctx - 1)
    pltpu.make_async_copy(log_in.at[others], log_in.at[others], log_recv).wait()
    logs = log_in[...].reshape(log_in.shape[0], HD)
    shares = jnp.exp2(logs - jnp.max(logs, axis=0, keepdims=True))
    shares = shares * (1.0 / jnp.sum(shares, axis=0, keepdims=True))
    columns = jnp.transpose(shares)
    pltpu.make_async_copy(part_in.at[others], part_in.at[others], part_recv).wait()
    joined = [jnp.zeros((8, HD), F32) for _ in range(rows // 8)]
    for i in range(n_ctx + 1):
        part = part_in[i].astype(F32)
        for v in range(rows // 8):
            joined[v] += part[8 * v : 8 * v + 8] * columns[8 * v : 8 * v + 8, i : i + 1]
    rows32[...] = jnp.concatenate(joined, axis=0)
    attention = jnp.concatenate(
        [rows32[pl.ds(s, GROUPS, stride=steps), :] for s in range(steps)], axis=0
    )
    att_all[me] = attention.astype(BF16)

    for d in others_list:
        pltpu.make_async_remote_copy(
            src_ref=att_all.at[me],
            dst_ref=att_all.at[me],
            send_sem=att_send,
            recv_sem=att_recv,
            device_id={"ctx": owner(d)},
            device_id_type=MESH,
        ).start()

    w_copy.wait()
    pltpu.make_async_copy(att_all.at[others], att_all.at[others], att_recv).wait()

    att32[...] = att_all[...].astype(F32).reshape(att32.shape)
    flat = jnp.concatenate(
        [att32[pl.ds(g, n_ctx * steps, stride=GROUPS), :].astype(BF16) for g in range(GROUPS)],
        axis=1,
    )
    mixed = jnp.dot(flat, w[...], preferred_element_type=F32)
    mix_out[...] = mixed.astype(BF16).reshape(mix_out.shape)

    for d in by_distance(n_head):
        to = lax.rem(my_head + d, n_head)
        pltpu.make_async_remote_copy(
            src_ref=mix_out.at[to],
            dst_ref=mix_in.at[my_head],
            send_sem=mix_send,
            recv_sem=mix_recv,
            device_id={"head": to},
            device_id_type=MESH,
        ).start()

    mix_in[my_head] = mix_out[my_head]
    other_heads = pl.ds(0, n_head - 1)
    pltpu.make_async_copy(mix_in.at[other_heads], mix_in.at[other_heads], mix_recv).wait()
    out_ref[...] = jnp.sum(mix_in[...].astype(F32), axis=0).astype(BF16)

    pltpu.make_async_copy(q_all.at[others], q_all.at[others], q_send).wait()
    pltpu.make_async_copy(part_out, part_out, part_send).wait()
    pltpu.make_async_copy(log_out, log_out, log_send).wait()
    pltpu.make_async_copy(att_all.at[others], att_all.at[others], att_send).wait()
    pltpu.make_async_copy(mix_out.at[other_heads], mix_out.at[other_heads], mix_send).wait()


def local(queries, kv_cache, new_kv, selected, out_weight, *, n_ctx, n_head):
    steps, _, width = queries.shape
    batch, pages = kv_cache.shape[:2]
    rows = steps * GROUPS
    columns = out_weight.shape[1]
    own = batch // n_head * steps
    dma = pltpu.SemaphoreType.DMA
    any_space = pl.BlockSpec(memory_space=pl.ANY)
    sel = jnp.transpose(selected, (0, 3, 2, 1))
    result = pl.pallas_call(
        functools.partial(kernel, n_ctx=n_ctx, n_head=n_head),
        out_shape=jax.ShapeDtypeStruct((own, columns), BF16),
        in_specs=[any_space] * 5,
        out_specs=pl.BlockSpec(memory_space=pltpu.VMEM),
        scratch_shapes=[
            pltpu.VMEM((steps, width), BF16),
            pltpu.VMEM((steps, 2, HD), BF16),
            pltpu.VMEM(sel.shape, jnp.int32),
            pltpu.VMEM(kv_cache.shape, BF16),
            pltpu.VMEM(out_weight.shape, BF16),
            pltpu.VMEM((rows, HD), F32),
            pltpu.VMEM((batch, rows, HD), BF16),
            pltpu.VMEM((batch, 8, pages * PAGE), F32),
            pltpu.VMEM((n_ctx - 1, rows, HD), BF16),
            pltpu.VMEM((n_ctx + 1, rows, HD), BF16),
            pltpu.VMEM((n_ctx - 1, 1, HD), F32),
            pltpu.VMEM((n_ctx + 8, 1, HD), F32),
            pltpu.VMEM((batch, rows, HD), BF16),
            pltpu.VMEM((batch * rows, HD), F32),
            pltpu.VMEM((n_head, own, columns), BF16),
            pltpu.VMEM((n_head, own, columns), BF16),
            dma((3,)),
            dma,
            dma,
            dma,
            dma((3,)),
            dma,
            dma,
            dma,
            dma,
            dma,
            dma,
            dma,
            dma,
        ],
        compiler_params=pltpu.CompilerParams(
            collective_id=0, has_side_effects=True, vmem_limit_bytes=56 * 1024 * 1024
        ),
    )(
        queries.reshape(steps, width),
        kv_cache,
        new_kv.reshape(steps, 2, HD),
        sel,
        out_weight,
    )
    return result.reshape(batch // n_head, steps, columns)


def solution(mesh):
    n_ctx, n_head = mesh.shape["ctx"], mesh.shape["head"]
    return jax.shard_map(
        functools.partial(local, n_ctx=n_ctx, n_head=n_head),
        mesh=mesh,
        in_specs=(
            P(None, "ctx", "head"),
            P(None, "ctx", None, None, "head"),
            P(None, "ctx", None, "head"),
            P(None, None, "head", None),
            P("head", "ctx"),
        ),
        out_specs=P("head", None, "ctx"),
        check_vma=False,
    )
```

```python
import functools
import math

import jax
import jax.numpy as jnp
from jax import lax
from jax.experimental import pallas as pl
from jax.experimental.pallas import tpu as pltpu
from jax.sharding import PartitionSpec as P

HQ = 64
KVH = 8
HD = 128
PAGE = 64
GROUPS = HQ // KVH

NEG = -1e30
EXPONENT = HD ** (-0.5) * math.log2(math.e)
BF16 = jnp.bfloat16
F32 = jnp.float32
MESH = pl.DeviceIdType.MESH


def axes_of(size):
    return {32: (4, 4, 2), 8: (2, 2, 2)}[size]


def displacements(size):
    nx, ny, nc = axes_of(size)
    every = [(x, y, c) for x in range(nx) for y in range(ny) for c in range(nc)][1:]
    return sorted(every, key=lambda d: -min(d[0], nx - d[0]) - min(d[1], ny - d[1]))


def half_of(x, y, c, size):
    nx, ny, _ = axes_of(size)
    return c * (nx * ny) + ((x + y) & 1) * (nx * ny // 2) + x * (ny // 2) + (y >> 1)


def log2_of(size):
    return size.bit_length() - 1


def joiner_of(half, size):
    nx, ny, nc = axes_of(size)
    chips = nx * ny
    c, place = half >> log2_of(chips), half & (chips - 1)
    odd, place = place >> log2_of(chips // 2), place & (chips // 2 - 1)
    x = place >> log2_of(ny // 2)
    y = 2 * (place & (ny // 2 - 1)) + ((x + odd) & 1)
    return (x * ny + y) * nc + c


def by_distance(size):
    return sorted(range(1, size), key=lambda d: -min(d, size - d))


def softmax_parts(queries, keys, values, masked):
    scores = [
        mask(lax.dot_general(q, k, (((1,), (1,)), ((), ())), preferred_element_type=F32))
        for q, k, mask in zip(queries, keys, masked)
    ]
    tops = [jnp.max(x, axis=-1, keepdims=True) for x in scores]
    expos = [jnp.exp2((x - top) * EXPONENT) for x, top in zip(scores, tops)]
    totals = [jnp.sum(x, axis=-1, keepdims=True) for x in expos]
    sums = [
        jnp.dot(x.astype(BF16), v, preferred_element_type=F32) for x, v in zip(expos, values)
    ]
    return [
        ((x * (1.0 / total)).astype(BF16), top * EXPONENT + jnp.log2(total))
        for x, top, total in zip(sums, tops, totals)
    ]


def as_row(column):
    lane = lax.broadcasted_iota(jnp.int32, (8, HD), 1)
    sublane = lax.broadcasted_iota(jnp.int32, (8, HD), 0)
    spread = jnp.zeros((8, HD), F32)
    for v in range(column.shape[0] // 8):
        spread = jnp.where(lane == sublane + 8 * v, column[8 * v : 8 * v + 8], spread)
    return jnp.sum(spread, axis=0, keepdims=True)


def kernel(
    q_hbm,
    kv_hbm,
    new_hbm,
    sel_hbm,
    w_hbm,
    out_ref,
    q_in,
    new_in,
    sel_in,
    kv,
    w,
    rows32,
    q_own,
    q_all,
    bias,
    fresh_out,
    fresh_log,
    part_out,
    part_in,
    log_out,
    log_in,
    att_own,
    att_all,
    att32,
    mix_out,
    mix_in,
    small_sem,
    kv_sem,
    w_sem,
    q_send,
    q_recv,
    part_send,
    part_recv,
    log_send,
    log_recv,
    fresh_send,
    att_send,
    att_recv,
    mix_send,
    mix_recv,
    *,
    n_ctx,
    n_head,
):
    steps = q_in.shape[0]
    pages = kv.shape[1]
    tokens = pages * PAGE
    rows = steps * GROUPS
    me = lax.axis_index("ctx")
    my_head = lax.axis_index("head")

    nx, ny, nc = axes_of(n_ctx)
    others_list = displacements(n_ctx)
    x, y, c = me // (ny * nc), (me // nc) & (ny - 1), me & (nc - 1)
    half = half_of(x, y, c, n_ctx)
    block = n_ctx // n_head
    groups = [(0, block), (block, n_ctx // 2), (n_ctx // 2, n_ctx)]
    groups = [group for group in groups if group[0] < group[1]]
    starts = [group[0] for group in groups]

    def owner(d):
        return (((x + d[0]) & (nx - 1)) * ny + ((y + d[1]) & (ny - 1))) * nc + ((c + d[2]) & (nc - 1))

    def group_of(sequence):
        return sum((sequence >= start).astype(jnp.int32) for start in starts[1:])

    def send(axis, here, to, src, dst, send_sem, recv_sem):
        @pl.when(here == to)
        def _():
            pltpu.make_async_copy(src, dst, recv_sem).start()

        @pl.when(here != to)
        def _():
            remote(axis, to, src, dst, send_sem, recv_sem).start()

    def remote(axis, to, src, dst, send_sem, recv_sem):
        return pltpu.make_async_remote_copy(
            src_ref=src,
            dst_ref=dst,
            send_sem=send_sem,
            recv_sem=recv_sem,
            device_id={axis: to},
            device_id_type=MESH,
        )

    def arrived(ref, sem):
        pltpu.make_async_copy(ref, ref, sem).wait()

    q_copy = pltpu.make_async_copy(q_hbm, q_in, small_sem.at[0])
    sel_copy = pltpu.make_async_copy(sel_hbm, sel_in, small_sem.at[1])
    new_copy = pltpu.make_async_copy(new_hbm, new_in, small_sem.at[2])
    w_copy = pltpu.make_async_copy(w_hbm, w, w_sem)
    q_copy.start()
    sel_copy.start()
    new_copy.start()

    barrier = pltpu.get_barrier_semaphore()

    for d in others_list:
        pl.semaphore_signal(barrier, inc=1, device_id={"ctx": owner(d)}, device_id_type=MESH)
    for d in by_distance(n_head):
        to = lax.rem(my_head + d, n_head)
        pl.semaphore_signal(barrier, inc=1, device_id={"head": to}, device_id_type=MESH)

    chunk = kv.shape[0] // 4
    for i in range(4):
        part = pl.ds(i * chunk, chunk)
        pltpu.make_async_copy(kv_hbm.at[part], kv.at[part], kv_sem).start()
    w_copy.start()

    q_copy.wait()
    for s in range(steps):
        for g in range(GROUPS):
            rows32[s * GROUPS + g : s * GROUPS + g + 1, :] = q_in[
                s : s + 1, g * HD : (g + 1) * HD
            ].astype(F32)
    q_own[...] = rows32[...].astype(BF16)

    pl.semaphore_wait(barrier, n_ctx - 1 + n_head - 1)

    q_sem = q_recv.at[group_of(me)]
    for d in others_list:
        remote("ctx", owner(d), q_own, q_all.at[me], q_send, q_sem).start()
    pltpu.make_async_copy(q_own, q_all.at[me], q_sem).start()

    sel_copy.wait()
    number = lax.broadcasted_iota(jnp.int32, (pages, n_ctx), 0) + me * pages
    from_b = lax.broadcasted_iota(jnp.int32, (n_ctx, n_ctx * rows), 0)
    to_lane = lax.broadcasted_iota(jnp.int32, (n_ctx, n_ctx * rows), 1)
    chosen = jnp.zeros((pages, n_ctx * rows), F32)
    for s in range(steps):
        hit = jnp.zeros((pages, n_ctx), F32)
        for j in range(sel_in.shape[1]):
            hit = jnp.where(sel_in[s, j] == number, 1.0, hit)
        spread = jnp.where(((to_lane >> log2_of(rows)) == from_b) & (((to_lane & (rows - 1)) >> 3) == s), 1.0, 0.0)
        chosen += jnp.dot(hit.astype(BF16), spread.astype(BF16), preferred_element_type=F32)
    page = lax.broadcasted_iota(jnp.int32, (pages, tokens), 0)
    token = lax.broadcasted_iota(jnp.int32, (pages, tokens), 1)
    expand = jnp.where((token >> 6) == page, 1.0, 0.0).astype(BF16)
    count = lax.dot_general(
        chosen.astype(BF16), expand, (((0,), (0,)), ((), ())), preferred_element_type=F32
    )
    bias[...] = ((count - 1.0) * -NEG).reshape(bias.shape)

    new_copy.wait()
    new_keys = jnp.concatenate(
        [new_in[:, 0].astype(F32), jnp.zeros((HD - steps, HD), F32)], axis=0
    ).astype(BF16)
    new_values = jnp.concatenate(
        [new_in[:, 1].astype(F32), jnp.zeros((HD - steps, HD), F32)], axis=0
    ).astype(BF16)
    step_of = lax.broadcasted_iota(jnp.int32, (rows, HD), 0) >> 3
    place = lax.broadcasted_iota(jnp.int32, (rows, HD), 1)

    def causal(scores):
        return jnp.where(place <= step_of, scores, NEG)

    def selected_of(b):
        def mask(scores):
            return scores + bias[b]

        return mask

    def keys_of(b):
        return kv[b, :, 0].reshape(tokens, HD)

    def values_of(b):
        return kv[b, :, 1].reshape(tokens, HD)

    own = q_own[...]
    ((normed, log),) = softmax_parts([own], [new_keys], [new_values], [causal])
    span = rows // 2
    phase = me >> log2_of(n_ctx // 2)
    fresh_to = [joiner_of((2 * me + h) & (n_ctx - 1), n_ctx) for h in range(2)]
    for h in range(2):
        fresh_out[h] = normed[h * span : (h + 1) * span]
        fresh_log[h] = as_row(log[h * span : (h + 1) * span])
    for h in range(2):
        send(
            "ctx",
            me,
            fresh_to[h],
            fresh_log.at[h],
            log_in.at[phase, n_ctx],
            fresh_send.at[h, 0],
            log_recv.at[phase],
        )
        send(
            "ctx",
            me,
            fresh_to[h],
            fresh_out.at[h],
            part_in.at[phase, n_ctx],
            fresh_send.at[h, 1],
            part_recv.at[phase],
        )
    for p in range(2):
        for i in range(n_ctx + 1, log_in.shape[1]):
            log_in[p, i] = jnp.full((1, HD), NEG, F32)
    arrived(kv, kv_sem)

    for i, (first, last) in enumerate(groups):
        arrived(q_all.at[pl.ds(0, last - first)], q_recv.at[i])
        results = softmax_parts(
            [q_all[b] for b in range(first, last)],
            [keys_of(b) for b in range(first, last)],
            [values_of(b) for b in range(first, last)],
            [selected_of(b) for b in range(first, last)],
        )
        for b, (normed, log) in zip(range(first, last), results):
            for h in range(2):
                part_out[2 * b + h] = normed[h * span : (h + 1) * span]
                log_out[2 * b + h] = as_row(log[h * span : (h + 1) * span])
        for u in range(2 * first, 2 * last):
            to, p = joiner_of(u % n_ctx, n_ctx), u // n_ctx
            send("ctx", me, to, log_out.at[u], log_in.at[p, me], log_send, log_recv.at[p])
            send("ctx", me, to, part_out.at[u], part_in.at[p, me], part_send, part_recv.at[p])

    for p in range(2):
        arrived(log_in.at[p, pl.ds(0, n_ctx + 1)], log_recv.at[p])
        logs = log_in[p].reshape(log_in.shape[1], HD)
        shares = jnp.exp2(logs - jnp.max(logs, axis=0, keepdims=True))
        shares = shares * (1.0 / jnp.sum(shares, axis=0, keepdims=True))
        columns = jnp.transpose(shares)
        arrived(part_in.at[p], part_recv.at[p])
        joined = [jnp.zeros((8, HD), F32) for _ in range(span // 8)]
        for i in range(n_ctx + 1):
            part = part_in[p, i].astype(F32)
            for v in range(span // 8):
                joined[v] += part[8 * v : 8 * v + 8] * columns[8 * v : 8 * v + 8, i : i + 1]
        att_own[p] = jnp.concatenate(joined, axis=0).astype(BF16)
        place = half + p * n_ctx
        att_sem = att_recv.at[group_of(place >> 1)]
        for d in others_list:
            remote("ctx", owner(d), att_own.at[p], att_all.at[place], att_send, att_sem).start()
        pltpu.make_async_copy(att_own.at[p], att_all.at[place], att_sem).start()

    w_copy.wait()
    for i, (first, last) in enumerate(groups):
        units = pl.ds(2 * first, 2 * (last - first))
        arrived(att_all.at[units], att_recv.at[i])
        base, count = first * rows, (last - first) * steps
        att32[base : base + count * GROUPS, :] = (
            att_all[2 * first : 2 * last].astype(F32).reshape(count * GROUPS, HD)
        )
        flat = jnp.concatenate(
            [att32[pl.ds(base + g, count, stride=GROUPS), :].astype(BF16) for g in range(GROUPS)],
            axis=1,
        )
        mixed = jnp.dot(flat, w[...], preferred_element_type=F32).astype(BF16)
        for to in range(first // block, last // block):
            row = (to * block - first) * steps
            mix_out[to] = mixed[row : row + block * steps]
        for to in range(first // block, last // block):
            send("head", my_head, to, mix_out.at[to], mix_in.at[my_head], mix_send, mix_recv)

    arrived(q_all.at[pl.ds(0, n_ctx - 1)], q_send)
    arrived(part_out.at[pl.ds(0, 2 * n_ctx - 2)], part_send)
    arrived(log_out.at[pl.ds(0, 2 * n_ctx - 2)], log_send)
    arrived(att_all.at[pl.ds(0, 2 * n_ctx - 2)], att_send)
    for h in range(2):

        @pl.when(me != fresh_to[h])
        def _():
            arrived(fresh_log.at[h], fresh_send.at[h, 0])
            arrived(fresh_out.at[h], fresh_send.at[h, 1])

    arrived(mix_in, mix_recv)
    out_ref[...] = jnp.sum(mix_in[...].astype(F32), axis=0).astype(BF16)
    arrived(mix_out.at[pl.ds(0, n_head - 1)], mix_send)


def local(queries, kv_cache, new_kv, selected, out_weight, *, n_ctx, n_head):
    steps, _, width = queries.shape
    batch, pages = kv_cache.shape[:2]
    rows = steps * GROUPS
    columns = out_weight.shape[1]
    own = batch // n_head * steps
    dma = pltpu.SemaphoreType.DMA
    any_space = pl.BlockSpec(memory_space=pl.ANY)
    sel = jnp.transpose(selected, (0, 3, 2, 1))
    result = pl.pallas_call(
        functools.partial(kernel, n_ctx=n_ctx, n_head=n_head),
        out_shape=jax.ShapeDtypeStruct((own, columns), BF16),
        in_specs=[any_space] * 5,
        out_specs=pl.BlockSpec(memory_space=pltpu.VMEM),
        scratch_shapes=[
            pltpu.VMEM((steps, width), BF16),
            pltpu.VMEM((steps, 2, HD), BF16),
            pltpu.VMEM(sel.shape, jnp.int32),
            pltpu.VMEM(kv_cache.shape, BF16),
            pltpu.VMEM(out_weight.shape, BF16),
            pltpu.VMEM((rows, HD), F32),
            pltpu.VMEM((rows, HD), BF16),
            pltpu.VMEM((batch, rows, HD), BF16),
            pltpu.VMEM((batch, rows, pages * PAGE), F32),
            pltpu.VMEM((2, rows // 2, HD), BF16),
            pltpu.VMEM((2, 1, HD), F32),
            pltpu.VMEM((2 * batch, rows // 2, HD), BF16),
            pltpu.VMEM((2, n_ctx + 1, rows // 2, HD), BF16),
            pltpu.VMEM((2 * batch, 1, HD), F32),
            pltpu.VMEM((2, n_ctx + 8, 1, HD), F32),
            pltpu.VMEM((2, rows // 2, HD), BF16),
            pltpu.VMEM((2 * batch, rows // 2, HD), BF16),
            pltpu.VMEM((batch * rows, HD), F32),
            pltpu.VMEM((n_head, own, columns), BF16),
            pltpu.VMEM((n_head, own, columns), BF16),
            dma((3,)),
            dma,
            dma,
            dma,
            dma((3,)),
            dma,
            dma((2,)),
            dma,
            dma((2,)),
            dma((2, 2)),
            dma,
            dma((3,)),
            dma,
            dma,
        ],
        compiler_params=pltpu.CompilerParams(
            collective_id=0, has_side_effects=True, vmem_limit_bytes=56 * 1024 * 1024
        ),
    )(
        queries.reshape(steps, width),
        kv_cache,
        new_kv.reshape(steps, 2, HD),
        sel,
        out_weight,
    )
    return result.reshape(batch // n_head, steps, columns)


def solution(mesh):
    n_ctx, n_head = mesh.shape["ctx"], mesh.shape["head"]
    return jax.shard_map(
        functools.partial(local, n_ctx=n_ctx, n_head=n_head),
        mesh=mesh,
        in_specs=(
            P(None, "ctx", "head"),
            P(None, "ctx", None, None, "head"),
            P(None, "ctx", None, "head"),
            P(None, None, "head", None),
            P("head", "ctx"),
        ),
        out_specs=P("head", None, "ctx"),
        check_vma=False,
    )
```

```python
import functools
import math

import jax
import jax.numpy as jnp
from jax import lax
from jax.experimental import pallas as pl
from jax.experimental.pallas import tpu as pltpu
from jax.sharding import PartitionSpec as P

HQ = 64
KVH = 8
HD = 128
PAGE = 64
GROUPS = HQ // KVH

NEG = -1e30
EXPONENT = HD ** (-0.5) * math.log2(math.e)
BF16 = jnp.bfloat16
F32 = jnp.float32
MESH = pl.DeviceIdType.MESH


def axes_of(size):
    return {32: (4, 4, 2), 8: (2, 2, 2)}[size]


def displacements(size):
    nx, ny, nc = axes_of(size)
    every = [(x, y, c) for x in range(nx) for y in range(ny) for c in range(nc)][1:]
    return sorted(every, key=lambda d: -min(d[0], nx - d[0]) - min(d[1], ny - d[1]))


def half_of(x, y, c, size):
    nx, ny, _ = axes_of(size)
    return c * (nx * ny) + ((x + y) & 1) * (nx * ny // 2) + x * (ny // 2) + (y >> 1)


def log2_of(size):
    return size.bit_length() - 1


def joiner_of(half, size):
    nx, ny, nc = axes_of(size)
    chips = nx * ny
    c, place = half >> log2_of(chips), half & (chips - 1)
    odd, place = place >> log2_of(chips // 2), place & (chips // 2 - 1)
    x = place >> log2_of(ny // 2)
    y = 2 * (place & (ny // 2 - 1)) + ((x + odd) & 1)
    return (x * ny + y) * nc + c


def by_distance(size):
    return sorted(range(1, size), key=lambda d: -min(d, size - d))


def softmax_parts(queries, keys, values, masked):
    scores = [
        mask(lax.dot_general(q, k, (((1,), (1,)), ((), ())), preferred_element_type=F32))
        for q, k, mask in zip(queries, keys, masked)
    ]
    tops = [jnp.max(x, axis=-1, keepdims=True) for x in scores]
    expos = [jnp.exp2((x - top) * EXPONENT) for x, top in zip(scores, tops)]
    totals = [jnp.sum(x, axis=-1, keepdims=True) for x in expos]
    sums = [
        jnp.dot(x.astype(BF16), v, preferred_element_type=F32) for x, v in zip(expos, values)
    ]
    return [
        ((x * (1.0 / total)).astype(BF16), top * EXPONENT + jnp.log2(total))
        for x, top, total in zip(sums, tops, totals)
    ]


def as_row(column):
    lane = lax.broadcasted_iota(jnp.int32, (8, HD), 1)
    sublane = lax.broadcasted_iota(jnp.int32, (8, HD), 0)
    spread = jnp.zeros((8, HD), F32)
    for v in range(column.shape[0] // 8):
        spread = jnp.where(lane == sublane + 8 * v, column[8 * v : 8 * v + 8], spread)
    return jnp.sum(spread, axis=0, keepdims=True)


def kernel(
    q_hbm,
    kv_hbm,
    new_hbm,
    sel_hbm,
    w_hbm,
    out_ref,
    q_in,
    new_in,
    sel_in,
    kv,
    w,
    rows32,
    q_own,
    q_all,
    bias,
    fresh_out,
    fresh_log,
    part_out,
    part_in,
    log_out,
    log_in,
    att_own,
    att_all,
    att32,
    mix_out,
    small_sem,
    kv_sem,
    w_sem,
    q_send,
    q_recv,
    part_send,
    part_recv,
    log_send,
    log_recv,
    fresh_send,
    att_send,
    att_recv,
    mix_send,
    mix_recv,
    *,
    n_ctx,
    n_head,
):
    steps = q_in.shape[0]
    pages = kv.shape[1]
    tokens = pages * PAGE
    rows = steps * GROUPS
    me = lax.axis_index("ctx")
    my_head = lax.axis_index("head")

    nx, ny, nc = axes_of(n_ctx)
    others_list = displacements(n_ctx)
    x, y, c = me // (ny * nc), (me // nc) & (ny - 1), me & (nc - 1)
    half = half_of(x, y, c, n_ctx)
    block = n_ctx // n_head
    bounds = sorted({0, block, 2 * block, n_ctx // 2, n_ctx})
    groups = list(zip(bounds, bounds[1:]))
    starts = [group[0] for group in groups]

    def owner(d):
        return (((x + d[0]) & (nx - 1)) * ny + ((y + d[1]) & (ny - 1))) * nc + ((c + d[2]) & (nc - 1))

    def group_of(sequence):
        return sum((sequence >= start).astype(jnp.int32) for start in starts[1:])

    def send(axis, here, to, src, dst, send_sem, recv_sem):
        @pl.when(here == to)
        def _():
            pltpu.make_async_copy(src, dst, recv_sem).start()

        @pl.when(here != to)
        def _():
            remote(axis, to, src, dst, send_sem, recv_sem).start()

    def remote(axis, to, src, dst, send_sem, recv_sem):
        return pltpu.make_async_remote_copy(
            src_ref=src,
            dst_ref=dst,
            send_sem=send_sem,
            recv_sem=recv_sem,
            device_id={axis: to},
            device_id_type=MESH,
        )

    def arrived(ref, sem):
        pltpu.make_async_copy(ref, ref, sem).wait()

    q_copy = pltpu.make_async_copy(q_hbm, q_in, small_sem.at[0])
    sel_copy = pltpu.make_async_copy(sel_hbm, sel_in, small_sem.at[1])
    new_copy = pltpu.make_async_copy(new_hbm, new_in, small_sem.at[2])
    w_copy = pltpu.make_async_copy(w_hbm, w, w_sem)
    q_copy.start()
    sel_copy.start()
    new_copy.start()

    barrier = pltpu.get_barrier_semaphore()

    for d in others_list:
        pl.semaphore_signal(barrier, inc=1, device_id={"ctx": owner(d)}, device_id_type=MESH)
    for d in by_distance(n_head):
        to = lax.rem(my_head + d, n_head)
        pl.semaphore_signal(barrier, inc=1, device_id={"head": to}, device_id_type=MESH)

    chunk = kv.shape[0] // 4
    for i in range(4):
        part = pl.ds(i * chunk, chunk)
        pltpu.make_async_copy(kv_hbm.at[part], kv.at[part], kv_sem).start()
    w_copy.start()

    q_copy.wait()
    for s in range(steps):
        for g in range(GROUPS):
            rows32[s * GROUPS + g : s * GROUPS + g + 1, :] = q_in[
                s : s + 1, g * HD : (g + 1) * HD
            ].astype(F32)
    q_own[...] = rows32[...].astype(BF16)

    pl.semaphore_wait(barrier, n_ctx - 1 + n_head - 1)

    q_sem = q_recv.at[group_of(me)]
    for d in others_list:
        remote("ctx", owner(d), q_own, q_all.at[me], q_send, q_sem).start()
    pltpu.make_async_copy(q_own, q_all.at[me], q_sem).start()

    sel_copy.wait()
    number = lax.broadcasted_iota(jnp.int32, (pages, n_ctx), 0) + me * pages
    from_b = lax.broadcasted_iota(jnp.int32, (n_ctx, n_ctx * rows), 0)
    to_lane = lax.broadcasted_iota(jnp.int32, (n_ctx, n_ctx * rows), 1)
    chosen = jnp.zeros((pages, n_ctx * rows), F32)
    for s in range(steps):
        hit = jnp.zeros((pages, n_ctx), F32)
        for j in range(sel_in.shape[1]):
            hit = jnp.where(sel_in[s, j] == number, 1.0, hit)
        spread = jnp.where(((to_lane >> log2_of(rows)) == from_b) & (((to_lane & (rows - 1)) >> 3) == s), 1.0, 0.0)
        chosen += jnp.dot(hit.astype(BF16), spread.astype(BF16), preferred_element_type=F32)
    page = lax.broadcasted_iota(jnp.int32, (pages, tokens), 0)
    token = lax.broadcasted_iota(jnp.int32, (pages, tokens), 1)
    expand = jnp.where((token >> 6) == page, 1.0, 0.0).astype(BF16)
    count = lax.dot_general(
        chosen.astype(BF16), expand, (((0,), (0,)), ((), ())), preferred_element_type=F32
    )
    bias[...] = ((count - 1.0) * -NEG).reshape(bias.shape)

    new_copy.wait()
    new_keys = jnp.concatenate(
        [new_in[:, 0].astype(F32), jnp.zeros((HD - steps, HD), F32)], axis=0
    ).astype(BF16)
    new_values = jnp.concatenate(
        [new_in[:, 1].astype(F32), jnp.zeros((HD - steps, HD), F32)], axis=0
    ).astype(BF16)
    step_of = lax.broadcasted_iota(jnp.int32, (rows, HD), 0) >> 3
    place = lax.broadcasted_iota(jnp.int32, (rows, HD), 1)

    def causal(scores):
        return jnp.where(place <= step_of, scores, NEG)

    def selected_of(b):
        def mask(scores):
            return scores + bias[b]

        return mask

    def keys_of(b):
        return kv[b, :, 0].reshape(tokens, HD)

    def values_of(b):
        return kv[b, :, 1].reshape(tokens, HD)

    own = q_own[...]
    ((normed, log),) = softmax_parts([own], [new_keys], [new_values], [causal])
    span = rows // 2
    phase = me >> log2_of(n_ctx // 2)
    fresh_to = [joiner_of((2 * me + h) & (n_ctx - 1), n_ctx) for h in range(2)]
    for h in range(2):
        fresh_out[h] = normed[h * span : (h + 1) * span]
        fresh_log[h] = as_row(log[h * span : (h + 1) * span])
    for h in range(2):
        send(
            "ctx",
            me,
            fresh_to[h],
            fresh_log.at[h],
            log_in.at[phase, n_ctx],
            fresh_send.at[h, 0],
            log_recv.at[phase],
        )
        send(
            "ctx",
            me,
            fresh_to[h],
            fresh_out.at[h],
            part_in.at[phase, n_ctx],
            fresh_send.at[h, 1],
            part_recv.at[phase],
        )
    for p in range(2):
        for i in range(n_ctx + 1, log_in.shape[1]):
            log_in[p, i] = jnp.full((1, HD), NEG, F32)
    arrived(kv, kv_sem)

    for i, (first, last) in enumerate(groups):
        arrived(q_all.at[pl.ds(0, last - first)], q_recv.at[i])
        results = softmax_parts(
            [q_all[b] for b in range(first, last)],
            [keys_of(b) for b in range(first, last)],
            [values_of(b) for b in range(first, last)],
            [selected_of(b) for b in range(first, last)],
        )
        for b, (normed, log) in zip(range(first, last), results):
            for h in range(2):
                part_out[2 * b + h] = normed[h * span : (h + 1) * span]
                log_out[2 * b + h] = as_row(log[h * span : (h + 1) * span])
        for u in range(2 * first, 2 * last):
            to, p = joiner_of(u % n_ctx, n_ctx), u // n_ctx
            send("ctx", me, to, log_out.at[u], log_in.at[p, me], log_send, log_recv.at[p])
            send("ctx", me, to, part_out.at[u], part_in.at[p, me], part_send, part_recv.at[p])

    for p in range(2):
        arrived(log_in.at[p, pl.ds(0, n_ctx + 1)], log_recv.at[p])
        logs = log_in[p].reshape(log_in.shape[1], HD)
        shares = jnp.exp2(logs - jnp.max(logs, axis=0, keepdims=True))
        shares = shares * (1.0 / jnp.sum(shares, axis=0, keepdims=True))
        columns = jnp.transpose(shares)
        arrived(part_in.at[p], part_recv.at[p])
        joined = [jnp.zeros((8, HD), F32) for _ in range(span // 8)]
        for i in range(n_ctx + 1):
            part = part_in[p, i].astype(F32)
            for v in range(span // 8):
                joined[v] += part[8 * v : 8 * v + 8] * columns[8 * v : 8 * v + 8, i : i + 1]
        att_own[p] = jnp.concatenate(joined, axis=0).astype(BF16)
        place = half + p * n_ctx
        att_sem = att_recv.at[group_of(place >> 1)]
        for d in others_list:
            remote("ctx", owner(d), att_own.at[p], att_all.at[place], att_send, att_sem).start()
        pltpu.make_async_copy(att_own.at[p], att_all.at[place], att_sem).start()

    w_copy.wait()
    for i, (first, last) in enumerate(groups):
        units = pl.ds(2 * first, 2 * (last - first))
        arrived(att_all.at[units], att_recv.at[i])
        base, count = first * rows, (last - first) * steps
        att32[base : base + count * GROUPS, :] = (
            att_all[2 * first : 2 * last].astype(F32).reshape(count * GROUPS, HD)
        )
        flat = jnp.concatenate(
            [att32[pl.ds(base + g, count, stride=GROUPS), :].astype(BF16) for g in range(GROUPS)],
            axis=1,
        )
        mixed = jnp.dot(flat, w[...], preferred_element_type=F32).astype(BF16)
        for to in range(first // block, last // block):
            row = (to * block - first) * steps
            mix_out[to] = mixed[row : row + block * steps]
        for to in range(first // block, last // block):
            send("head", my_head, to, mix_out.at[to], out_ref.at[my_head], mix_send, mix_recv)

    arrived(q_all.at[pl.ds(0, n_ctx - 1)], q_send)
    arrived(part_out.at[pl.ds(0, 2 * n_ctx - 2)], part_send)
    arrived(log_out.at[pl.ds(0, 2 * n_ctx - 2)], log_send)
    arrived(att_all.at[pl.ds(0, 2 * n_ctx - 2)], att_send)
    for h in range(2):

        @pl.when(me != fresh_to[h])
        def _():
            arrived(fresh_log.at[h], fresh_send.at[h, 0])
            arrived(fresh_out.at[h], fresh_send.at[h, 1])

    arrived(mix_out.at[pl.ds(0, n_head - 1)], mix_send)
    arrived(out_ref, mix_recv)


def local(queries, kv_cache, new_kv, selected, out_weight, *, n_ctx, n_head):
    steps, _, width = queries.shape
    batch, pages = kv_cache.shape[:2]
    rows = steps * GROUPS
    columns = out_weight.shape[1]
    own = batch // n_head * steps
    dma = pltpu.SemaphoreType.DMA
    any_space = pl.BlockSpec(memory_space=pl.ANY)
    sel = jnp.transpose(selected, (0, 3, 2, 1))
    result = pl.pallas_call(
        functools.partial(kernel, n_ctx=n_ctx, n_head=n_head),
        out_shape=jax.ShapeDtypeStruct((n_head, own, columns), BF16),
        in_specs=[any_space] * 5,
        out_specs=any_space,
        scratch_shapes=[
            pltpu.VMEM((steps, width), BF16),
            pltpu.VMEM((steps, 2, HD), BF16),
            pltpu.VMEM(sel.shape, jnp.int32),
            pltpu.VMEM(kv_cache.shape, BF16),
            pltpu.VMEM(out_weight.shape, BF16),
            pltpu.VMEM((rows, HD), F32),
            pltpu.VMEM((rows, HD), BF16),
            pltpu.VMEM((batch, rows, HD), BF16),
            pltpu.VMEM((batch, rows, pages * PAGE), F32),
            pltpu.VMEM((2, rows // 2, HD), BF16),
            pltpu.VMEM((2, 1, HD), F32),
            pltpu.VMEM((2 * batch, rows // 2, HD), BF16),
            pltpu.VMEM((2, n_ctx + 1, rows // 2, HD), BF16),
            pltpu.VMEM((2 * batch, 1, HD), F32),
            pltpu.VMEM((2, n_ctx + 8, 1, HD), F32),
            pltpu.VMEM((2, rows // 2, HD), BF16),
            pltpu.VMEM((2 * batch, rows // 2, HD), BF16),
            pltpu.VMEM((batch * rows, HD), F32),
            pltpu.VMEM((n_head, own, columns), BF16),
            dma((3,)),
            dma,
            dma,
            dma,
            dma((4,)),
            dma,
            dma((2,)),
            dma,
            dma((2,)),
            dma((2, 2)),
            dma,
            dma((4,)),
            dma,
            dma,
        ],
        compiler_params=pltpu.CompilerParams(
            collective_id=0, has_side_effects=True, vmem_limit_bytes=56 * 1024 * 1024
        ),
    )(
        queries.reshape(steps, width),
        kv_cache,
        new_kv.reshape(steps, 2, HD),
        sel,
        out_weight,
    )
    result = jnp.sum(result.astype(F32), axis=0).astype(BF16)
    return result.reshape(batch // n_head, steps, columns)


def solution(mesh):
    n_ctx, n_head = mesh.shape["ctx"], mesh.shape["head"]
    return jax.shard_map(
        functools.partial(local, n_ctx=n_ctx, n_head=n_head),
        mesh=mesh,
        in_specs=(
            P(None, "ctx", "head"),
            P(None, "ctx", None, None, "head"),
            P(None, "ctx", None, "head"),
            P(None, None, "head", None),
            P("head", "ctx"),
        ),
        out_specs=P("head", None, "ctx"),
        check_vma=False,
    )
```

```python
import functools
import math

import jax
import jax.numpy as jnp
from jax import lax
from jax.experimental import pallas as pl
from jax.experimental.pallas import tpu as pltpu
from jax.sharding import PartitionSpec as P

HQ = 64
KVH = 8
HD = 128
PAGE = 64
GROUPS = HQ // KVH

NEG = -1e30
EXPONENT = HD ** (-0.5) * math.log2(math.e)
BF16 = jnp.bfloat16
F32 = jnp.float32
MESH = pl.DeviceIdType.MESH


def axes_of(size):
    return {32: (4, 4, 2), 8: (2, 2, 2)}[size]


def displacements(size):
    nx, ny, nc = axes_of(size)
    every = [(x, y, c) for x in range(nx) for y in range(ny) for c in range(nc)][1:]
    return sorted(every, key=lambda d: -min(d[0], nx - d[0]) - min(d[1], ny - d[1]))


def half_of(x, y, c, size):
    nx, ny, _ = axes_of(size)
    return c * (nx * ny) + ((x + y) & 1) * (nx * ny // 2) + x * (ny // 2) + (y >> 1)


def log2_of(size):
    return size.bit_length() - 1


def joiner_of(half, size):
    nx, ny, nc = axes_of(size)
    chips = nx * ny
    c, place = half >> log2_of(chips), half & (chips - 1)
    odd, place = place >> log2_of(chips // 2), place & (chips // 2 - 1)
    x = place >> log2_of(ny // 2)
    y = 2 * (place & (ny // 2 - 1)) + ((x + odd) & 1)
    return (x * ny + y) * nc + c


def by_distance(size):
    return sorted(range(1, size), key=lambda d: -min(d, size - d))


def softmax_parts(queries, keys, values, masked):
    scores = [
        mask(lax.dot_general(q, k, (((1,), (1,)), ((), ())), preferred_element_type=F32))
        for q, k, mask in zip(queries, keys, masked)
    ]
    tops = [jnp.max(x, axis=-1, keepdims=True) for x in scores]
    expos = [jnp.exp2((x - top) * EXPONENT) for x, top in zip(scores, tops)]
    totals = [jnp.sum(x, axis=-1, keepdims=True) for x in expos]
    sums = [
        jnp.dot(x.astype(BF16), v, preferred_element_type=F32) for x, v in zip(expos, values)
    ]
    return [
        ((x * (1.0 / total)).astype(BF16), top * EXPONENT + jnp.log2(total))
        for x, top, total in zip(sums, tops, totals)
    ]


def as_row(column):
    lane = lax.broadcasted_iota(jnp.int32, (8, HD), 1)
    sublane = lax.broadcasted_iota(jnp.int32, (8, HD), 0)
    spread = jnp.zeros((8, HD), F32)
    for v in range(column.shape[0] // 8):
        spread = jnp.where(lane == sublane + 8 * v, column[8 * v : 8 * v + 8], spread)
    return jnp.sum(spread, axis=0, keepdims=True)


def kernel(
    q_hbm,
    kv_hbm,
    new_hbm,
    sel_hbm,
    w_hbm,
    out_ref,
    q_in,
    new_in,
    sel_in,
    kv,
    w,
    rows32,
    q_own,
    q_all,
    bias,
    fresh_out,
    fresh_log,
    part_out,
    part_in,
    log_out,
    log_in,
    att_own,
    att_all,
    att32,
    mix_out,
    mix_in,
    small_sem,
    kv_sem,
    w_sem,
    q_send,
    q_recv,
    part_send,
    part_recv,
    log_send,
    log_recv,
    fresh_send,
    att_send,
    att_recv,
    mix_send,
    mix_recv,
    *,
    n_ctx,
    n_head,
):
    steps = q_in.shape[0]
    pages = kv.shape[1]
    tokens = pages * PAGE
    rows = steps * GROUPS
    me = lax.axis_index("ctx")
    my_head = lax.axis_index("head")

    nx, ny, nc = axes_of(n_ctx)
    others_list = displacements(n_ctx)
    x, y, c = me // (ny * nc), (me // nc) & (ny - 1), me & (nc - 1)
    half = half_of(x, y, c, n_ctx)
    block = n_ctx // n_head
    bounds = sorted({0, block, 2 * block, n_ctx // 2, n_ctx})
    groups = list(zip(bounds, bounds[1:]))
    starts = [group[0] for group in groups]

    def owner(d):
        return (((x + d[0]) & (nx - 1)) * ny + ((y + d[1]) & (ny - 1))) * nc + ((c + d[2]) & (nc - 1))

    def group_of(sequence):
        return sum((sequence >= start).astype(jnp.int32) for start in starts[1:])

    def send(axis, here, to, src, dst, send_sem, recv_sem):
        @pl.when(here == to)
        def _():
            pltpu.make_async_copy(src, dst, recv_sem).start()

        @pl.when(here != to)
        def _():
            remote(axis, to, src, dst, send_sem, recv_sem).start()

    def remote(axis, to, src, dst, send_sem, recv_sem):
        return pltpu.make_async_remote_copy(
            src_ref=src,
            dst_ref=dst,
            send_sem=send_sem,
            recv_sem=recv_sem,
            device_id={axis: to},
            device_id_type=MESH,
        )

    def arrived(ref, sem):
        pltpu.make_async_copy(ref, ref, sem).wait()

    q_copy = pltpu.make_async_copy(q_hbm, q_in, small_sem.at[0])
    sel_copy = pltpu.make_async_copy(sel_hbm, sel_in, small_sem.at[1])
    new_copy = pltpu.make_async_copy(new_hbm, new_in, small_sem.at[2])
    w_copy = pltpu.make_async_copy(w_hbm, w, w_sem)
    q_copy.start()
    sel_copy.start()
    new_copy.start()

    barrier = pltpu.get_barrier_semaphore()

    for d in others_list:
        pl.semaphore_signal(barrier, inc=1, device_id={"ctx": owner(d)}, device_id_type=MESH)
    for d in by_distance(n_head):
        to = lax.rem(my_head + d, n_head)
        pl.semaphore_signal(barrier, inc=1, device_id={"head": to}, device_id_type=MESH)

    chunk = kv.shape[0] // 4
    for i in range(4):
        part = pl.ds(i * chunk, chunk)
        pltpu.make_async_copy(kv_hbm.at[part], kv.at[part], kv_sem).start()
    w_copy.start()

    q_copy.wait()
    for s in range(steps):
        for g in range(GROUPS):
            rows32[s * GROUPS + g : s * GROUPS + g + 1, :] = q_in[
                s : s + 1, g * HD : (g + 1) * HD
            ].astype(F32)
    q_own[...] = rows32[...].astype(BF16)

    pl.semaphore_wait(barrier, n_ctx - 1 + n_head - 1)

    q_sem = q_recv.at[group_of(me)]
    for d in others_list:
        remote("ctx", owner(d), q_own, q_all.at[me], q_send, q_sem).start()
    pltpu.make_async_copy(q_own, q_all.at[me], q_sem).start()

    sel_copy.wait()
    number = lax.broadcasted_iota(jnp.int32, (pages, n_ctx), 0) + me * pages
    from_b = lax.broadcasted_iota(jnp.int32, (n_ctx, n_ctx * rows), 0)
    to_lane = lax.broadcasted_iota(jnp.int32, (n_ctx, n_ctx * rows), 1)
    chosen = jnp.zeros((pages, n_ctx * rows), F32)
    for s in range(steps):
        hit = jnp.zeros((pages, n_ctx), F32)
        for j in range(sel_in.shape[1]):
            hit = jnp.where(sel_in[s, j] == number, 1.0, hit)
        spread = jnp.where(((to_lane >> log2_of(rows)) == from_b) & (((to_lane & (rows - 1)) >> 3) == s), 1.0, 0.0)
        chosen += jnp.dot(hit.astype(BF16), spread.astype(BF16), preferred_element_type=F32)
    page = lax.broadcasted_iota(jnp.int32, (pages, tokens), 0)
    token = lax.broadcasted_iota(jnp.int32, (pages, tokens), 1)
    expand = jnp.where((token >> 6) == page, 1.0, 0.0).astype(BF16)
    count = lax.dot_general(
        chosen.astype(BF16), expand, (((0,), (0,)), ((), ())), preferred_element_type=F32
    )
    bias[...] = ((count - 1.0) * -NEG).reshape(bias.shape)

    new_copy.wait()
    new_keys = jnp.concatenate(
        [new_in[:, 0].astype(F32), jnp.zeros((HD - steps, HD), F32)], axis=0
    ).astype(BF16)
    new_values = jnp.concatenate(
        [new_in[:, 1].astype(F32), jnp.zeros((HD - steps, HD), F32)], axis=0
    ).astype(BF16)
    step_of = lax.broadcasted_iota(jnp.int32, (rows, HD), 0) >> 3
    place = lax.broadcasted_iota(jnp.int32, (rows, HD), 1)

    def causal(scores):
        return jnp.where(place <= step_of, scores, NEG)

    def selected_of(b):
        def mask(scores):
            return scores + bias[b]

        return mask

    def keys_of(b):
        return kv[b, :, 0].reshape(tokens, HD)

    def values_of(b):
        return kv[b, :, 1].reshape(tokens, HD)

    own = q_own[...]
    ((normed, log),) = softmax_parts([own], [new_keys], [new_values], [causal])
    span = rows // 2
    phase = me >> log2_of(n_ctx // 2)
    fresh_to = [joiner_of((2 * me + h) & (n_ctx - 1), n_ctx) for h in range(2)]
    for h in range(2):
        fresh_out[h] = normed[h * span : (h + 1) * span]
        fresh_log[h] = as_row(log[h * span : (h + 1) * span])
    for h in range(2):
        send(
            "ctx",
            me,
            fresh_to[h],
            fresh_log.at[h],
            log_in.at[phase, n_ctx],
            fresh_send.at[h, 0],
            log_recv.at[phase],
        )
        send(
            "ctx",
            me,
            fresh_to[h],
            fresh_out.at[h],
            part_in.at[phase, n_ctx],
            fresh_send.at[h, 1],
            part_recv.at[phase],
        )
    for p in range(2):
        for i in range(n_ctx + 1, log_in.shape[1]):
            log_in[p, i] = jnp.full((1, HD), NEG, F32)
    arrived(kv, kv_sem)

    for i, (first, last) in enumerate(groups):
        arrived(q_all.at[pl.ds(0, last - first)], q_recv.at[i])
        results = softmax_parts(
            [q_all[b] for b in range(first, last)],
            [keys_of(b) for b in range(first, last)],
            [values_of(b) for b in range(first, last)],
            [selected_of(b) for b in range(first, last)],
        )
        for b, (normed, log) in zip(range(first, last), results):
            for h in range(2):
                part_out[2 * b + h] = normed[h * span : (h + 1) * span]
                log_out[2 * b + h] = as_row(log[h * span : (h + 1) * span])
        for u in range(2 * first, 2 * last):
            to, p = joiner_of(u % n_ctx, n_ctx), u // n_ctx
            send("ctx", me, to, log_out.at[u], log_in.at[p, me], log_send, log_recv.at[p])
            send("ctx", me, to, part_out.at[u], part_in.at[p, me], part_send, part_recv.at[p])

    for p in range(2):
        arrived(log_in.at[p, pl.ds(0, n_ctx + 1)], log_recv.at[p])
        logs = log_in[p].reshape(log_in.shape[1], HD)
        shares = jnp.exp2(logs - jnp.max(logs, axis=0, keepdims=True))
        shares = shares * (1.0 / jnp.sum(shares, axis=0, keepdims=True))
        columns = jnp.transpose(shares)
        arrived(part_in.at[p], part_recv.at[p])
        joined = [jnp.zeros((8, HD), F32) for _ in range(span // 8)]
        for i in range(n_ctx + 1):
            part = part_in[p, i].astype(F32)
            for v in range(span // 8):
                joined[v] += part[8 * v : 8 * v + 8] * columns[8 * v : 8 * v + 8, i : i + 1]
        att_own[p] = jnp.concatenate(joined, axis=0).astype(BF16)
        place = half + p * n_ctx
        att_sem = att_recv.at[group_of(place >> 1)]
        for d in others_list:
            remote("ctx", owner(d), att_own.at[p], att_all.at[place], att_send, att_sem).start()
        pltpu.make_async_copy(att_own.at[p], att_all.at[place], att_sem).start()

    w_copy.wait()
    for i, (first, last) in enumerate(groups):
        units = pl.ds(2 * first, 2 * (last - first))
        arrived(att_all.at[units], att_recv.at[i])
        base, count = first * rows, (last - first) * steps
        att32[base : base + count * GROUPS, :] = (
            att_all[2 * first : 2 * last].astype(F32).reshape(count * GROUPS, HD)
        )
        flat = jnp.concatenate(
            [att32[pl.ds(base + g, count, stride=GROUPS), :].astype(BF16) for g in range(GROUPS)],
            axis=1,
        )
        mixed = jnp.dot(flat, w[...], preferred_element_type=F32).astype(BF16)
        for to in range(first // block, last // block):
            row = (to * block - first) * steps
            mix_out[to] = mixed[row : row + block * steps]
        for to in range(first // block, last // block):
            send("head", my_head, to, mix_out.at[to], mix_in.at[my_head], mix_send, mix_recv)

    arrived(q_all.at[pl.ds(0, n_ctx - 1)], q_send)
    arrived(part_out.at[pl.ds(0, 2 * n_ctx - 2)], part_send)
    arrived(log_out.at[pl.ds(0, 2 * n_ctx - 2)], log_send)
    arrived(att_all.at[pl.ds(0, 2 * n_ctx - 2)], att_send)
    for h in range(2):

        @pl.when(me != fresh_to[h])
        def _():
            arrived(fresh_log.at[h], fresh_send.at[h, 0])
            arrived(fresh_out.at[h], fresh_send.at[h, 1])

    arrived(mix_out.at[pl.ds(0, n_head - 1)], mix_send)
    arrived(mix_in, mix_recv)
    total = jnp.sum(mix_in[...].astype(F32), axis=0)
    for i in range(out_ref.shape[0]):
        out_ref[i] = total[i * steps : (i + 1) * steps].astype(BF16)


def local(queries, kv_cache, new_kv, selected, out_weight, *, n_ctx, n_head):
    steps, _, width = queries.shape
    batch, pages = kv_cache.shape[:2]
    rows = steps * GROUPS
    columns = out_weight.shape[1]
    own = batch // n_head * steps
    dma = pltpu.SemaphoreType.DMA
    any_space = pl.BlockSpec(memory_space=pl.ANY)
    sel = jnp.transpose(selected, (0, 3, 2, 1))
    result = pl.pallas_call(
        functools.partial(kernel, n_ctx=n_ctx, n_head=n_head),
        out_shape=pltpu.VMEM((own // steps, steps, columns), BF16),
        in_specs=[any_space] * 5,
        out_specs=pl.BlockSpec(memory_space=pltpu.VMEM),
        scratch_shapes=[
            pltpu.VMEM((steps, width), BF16),
            pltpu.VMEM((steps, 2, HD), BF16),
            pltpu.VMEM(sel.shape, jnp.int32),
            pltpu.VMEM(kv_cache.shape, BF16),
            pltpu.VMEM(out_weight.shape, BF16),
            pltpu.VMEM((rows, HD), F32),
            pltpu.VMEM((rows, HD), BF16),
            pltpu.VMEM((batch, rows, HD), BF16),
            pltpu.VMEM((batch, rows, pages * PAGE), F32),
            pltpu.VMEM((2, rows // 2, HD), BF16),
            pltpu.VMEM((2, 1, HD), F32),
            pltpu.VMEM((2 * batch, rows // 2, HD), BF16),
            pltpu.VMEM((2, n_ctx + 1, rows // 2, HD), BF16),
            pltpu.VMEM((2 * batch, 1, HD), F32),
            pltpu.VMEM((2, n_ctx + 8, 1, HD), F32),
            pltpu.VMEM((2, rows // 2, HD), BF16),
            pltpu.VMEM((2 * batch, rows // 2, HD), BF16),
            pltpu.VMEM((batch * rows, HD), F32),
            pltpu.VMEM((n_head, own, columns), BF16),
            pltpu.VMEM((n_head, own, columns), BF16),
            dma((3,)),
            dma,
            dma,
            dma,
            dma((4,)),
            dma,
            dma((2,)),
            dma,
            dma((2,)),
            dma((2, 2)),
            dma,
            dma((4,)),
            dma,
            dma,
        ],
        compiler_params=pltpu.CompilerParams(
            collective_id=0, has_side_effects=True, vmem_limit_bytes=56 * 1024 * 1024
        ),
    )(
        queries.reshape(steps, width),
        kv_cache,
        new_kv.reshape(steps, 2, HD),
        sel,
        out_weight,
    )
    return result


def solution(mesh):
    n_ctx, n_head = mesh.shape["ctx"], mesh.shape["head"]
    return jax.shard_map(
        functools.partial(local, n_ctx=n_ctx, n_head=n_head),
        mesh=mesh,
        in_specs=(
            P(None, "ctx", "head"),
            P(None, "ctx", None, None, "head"),
            P(None, "ctx", None, "head"),
            P(None, None, "head", None),
            P("head", "ctx"),
        ),
        out_specs=P("head", None, "ctx"),
        check_vma=False,
    )
```

```python
import functools
import math

import jax
import jax.numpy as jnp
from jax import lax
from jax.experimental import pallas as pl
from jax.experimental.pallas import tpu as pltpu
from jax.sharding import PartitionSpec as P

HQ = 64
KVH = 8
HD = 128
PAGE = 64
GROUPS = HQ // KVH

NEG = -1e30
EXPONENT = HD ** (-0.5) * math.log2(math.e)
BF16 = jnp.bfloat16
F32 = jnp.float32
MESH = pl.DeviceIdType.MESH


def axes_of(size):
    return {32: (4, 4, 2), 8: (2, 2, 2)}[size]


def displacements(size):
    nx, ny, nc = axes_of(size)
    every = [(x, y, c) for x in range(nx) for y in range(ny) for c in range(nc)][1:]
    return sorted(every, key=lambda d: -min(d[0], nx - d[0]) - min(d[1], ny - d[1]))


def half_of(x, y, c, size):
    nx, ny, _ = axes_of(size)
    return c * (nx * ny) + ((x + y) & 1) * (nx * ny // 2) + x * (ny // 2) + (y >> 1)


def log2_of(size):
    return size.bit_length() - 1


def joiner_of(half, size):
    nx, ny, nc = axes_of(size)
    chips = nx * ny
    c, place = half >> log2_of(chips), half & (chips - 1)
    odd, place = place >> log2_of(chips // 2), place & (chips // 2 - 1)
    x = place >> log2_of(ny // 2)
    y = 2 * (place & (ny // 2 - 1)) + ((x + odd) & 1)
    return (x * ny + y) * nc + c


def by_distance(size):
    return sorted(range(1, size), key=lambda d: -min(d, size - d))


def softmax_parts(queries, keys, values, masked):
    scores = [
        mask(lax.dot_general(q, k, (((1,), (1,)), ((), ())), preferred_element_type=F32))
        for q, k, mask in zip(queries, keys, masked)
    ]
    tops = [jnp.max(x, axis=-1, keepdims=True) for x in scores]
    expos = [jnp.exp2((x - top) * EXPONENT) for x, top in zip(scores, tops)]
    totals = [jnp.sum(x, axis=-1, keepdims=True) for x in expos]
    sums = [
        jnp.dot(x.astype(BF16), v, preferred_element_type=F32) for x, v in zip(expos, values)
    ]
    return [
        ((x * (1.0 / total)).astype(BF16), top * EXPONENT + jnp.log2(total))
        for x, top, total in zip(sums, tops, totals)
    ]


def as_row(column):
    lane = lax.broadcasted_iota(jnp.int32, (8, HD), 1)
    sublane = lax.broadcasted_iota(jnp.int32, (8, HD), 0)
    spread = jnp.zeros((8, HD), F32)
    for v in range(column.shape[0] // 8):
        spread = jnp.where(lane == sublane + 8 * v, column[8 * v : 8 * v + 8], spread)
    return jnp.sum(spread, axis=0, keepdims=True)


def kernel(
    q_hbm,
    kv_hbm,
    new_hbm,
    sel_hbm,
    w_hbm,
    out_ref,
    q_in,
    new_in,
    sel_in,
    kv,
    w,
    rows32,
    q_own,
    q_all,
    bias,
    fresh_out,
    fresh_log,
    part_out,
    part_in,
    log_out,
    log_in,
    att_own,
    att_all,
    att32,
    mix_out,
    mix_in,
    small_sem,
    kv_sem,
    w_sem,
    q_send,
    q_recv,
    part_send,
    part_recv,
    log_send,
    log_recv,
    fresh_send,
    att_send,
    att_recv,
    mix_send,
    mix_recv,
    *,
    n_ctx,
    n_head,
):
    steps = q_in.shape[0]
    pages = kv.shape[1]
    tokens = pages * PAGE
    rows = steps * GROUPS
    me = lax.axis_index("ctx")
    my_head = lax.axis_index("head")

    nx, ny, nc = axes_of(n_ctx)
    others_list = displacements(n_ctx)
    x, y, c = me // (ny * nc), (me // nc) & (ny - 1), me & (nc - 1)
    half = half_of(x, y, c, n_ctx)
    block = n_ctx // n_head
    bounds = sorted({0, block, 2 * block, n_ctx // 2, n_ctx})
    groups = list(zip(bounds, bounds[1:]))
    starts = [group[0] for group in groups]

    def owner(d):
        return (((x + d[0]) & (nx - 1)) * ny + ((y + d[1]) & (ny - 1))) * nc + ((c + d[2]) & (nc - 1))

    def group_of(sequence):
        return sum((sequence >= start).astype(jnp.int32) for start in starts[1:])

    def send(axis, here, to, src, dst, send_sem, recv_sem):
        @pl.when(here == to)
        def _():
            pltpu.make_async_copy(src, dst, recv_sem).start()

        @pl.when(here != to)
        def _():
            remote(axis, to, src, dst, send_sem, recv_sem).start()

    def remote(axis, to, src, dst, send_sem, recv_sem):
        return pltpu.make_async_remote_copy(
            src_ref=src,
            dst_ref=dst,
            send_sem=send_sem,
            recv_sem=recv_sem,
            device_id={axis: to},
            device_id_type=MESH,
        )

    def arrived(ref, sem):
        pltpu.make_async_copy(ref, ref, sem).wait()

    q_copy = pltpu.make_async_copy(q_hbm, q_in, small_sem.at[0])
    sel_copy = pltpu.make_async_copy(sel_hbm, sel_in, small_sem.at[1])
    new_copy = pltpu.make_async_copy(new_hbm, new_in, small_sem.at[2])
    w_copy = pltpu.make_async_copy(w_hbm, w, w_sem)
    q_copy.start()
    sel_copy.start()
    new_copy.start()

    barrier = pltpu.get_barrier_semaphore()

    for d in others_list:
        pl.semaphore_signal(barrier, inc=1, device_id={"ctx": owner(d)}, device_id_type=MESH)
    for d in by_distance(n_head):
        to = lax.rem(my_head + d, n_head)
        pl.semaphore_signal(barrier, inc=1, device_id={"head": to}, device_id_type=MESH)

    chunk = kv.shape[0] // 4
    for i in range(4):
        part = pl.ds(i * chunk, chunk)
        pltpu.make_async_copy(kv_hbm.at[part], kv.at[part], kv_sem).start()
    w_copy.start()

    q_copy.wait()
    for s in range(steps):
        for g in range(GROUPS):
            rows32[s * GROUPS + g : s * GROUPS + g + 1, :] = q_in[
                s : s + 1, g * HD : (g + 1) * HD
            ].astype(F32)
    q_own[...] = rows32[...].astype(BF16)

    pl.semaphore_wait(barrier, n_ctx - 1 + n_head - 1)

    q_sem = q_recv.at[group_of(me)]
    for d in others_list:
        remote("ctx", owner(d), q_own, q_all.at[me], q_send, q_sem).start()
    pltpu.make_async_copy(q_own, q_all.at[me], q_sem).start()

    sel_copy.wait()
    number = lax.broadcasted_iota(jnp.int32, (pages, n_ctx), 0) + me * pages
    from_b = lax.broadcasted_iota(jnp.int32, (n_ctx, n_ctx * rows), 0)
    to_lane = lax.broadcasted_iota(jnp.int32, (n_ctx, n_ctx * rows), 1)
    chosen = jnp.zeros((pages, n_ctx * rows), F32)
    for s in range(steps):
        hit = jnp.zeros((pages, n_ctx), F32)
        for j in range(sel_in.shape[1]):
            hit = jnp.where(sel_in[s, j] == number, 1.0, hit)
        spread = jnp.where(((to_lane >> log2_of(rows)) == from_b) & (((to_lane & (rows - 1)) >> 3) == s), 1.0, 0.0)
        chosen += jnp.dot(hit.astype(BF16), spread.astype(BF16), preferred_element_type=F32)
    page = lax.broadcasted_iota(jnp.int32, (pages, tokens), 0)
    token = lax.broadcasted_iota(jnp.int32, (pages, tokens), 1)
    expand = jnp.where((token >> 6) == page, 1.0, 0.0).astype(BF16)
    count = lax.dot_general(
        chosen.astype(BF16), expand, (((0,), (0,)), ((), ())), preferred_element_type=F32
    )
    bias[...] = ((count - 1.0) * -NEG).reshape(bias.shape)

    new_copy.wait()
    new_keys = jnp.concatenate(
        [new_in[:, 0].astype(F32), jnp.zeros((HD - steps, HD), F32)], axis=0
    ).astype(BF16)
    new_values = jnp.concatenate(
        [new_in[:, 1].astype(F32), jnp.zeros((HD - steps, HD), F32)], axis=0
    ).astype(BF16)
    step_of = lax.broadcasted_iota(jnp.int32, (rows, HD), 0) >> 3
    place = lax.broadcasted_iota(jnp.int32, (rows, HD), 1)

    def causal(scores):
        return jnp.where(place <= step_of, scores, NEG)

    def selected_of(b):
        def mask(scores):
            return scores + bias[b]

        return mask

    def keys_of(b):
        return kv[b, :, 0].reshape(tokens, HD)

    def values_of(b):
        return kv[b, :, 1].reshape(tokens, HD)

    own = q_own[...]
    ((normed, log),) = softmax_parts([own], [new_keys], [new_values], [causal])
    span = rows // 2
    phase = me >> log2_of(n_ctx // 2)
    fresh_to = [joiner_of((2 * me + h) & (n_ctx - 1), n_ctx) for h in range(2)]
    for h in range(2):
        fresh_out[h] = normed[h * span : (h + 1) * span]
        fresh_log[h] = as_row(log[h * span : (h + 1) * span])
    for h in range(2):
        send(
            "ctx",
            me,
            fresh_to[h],
            fresh_log.at[h],
            log_in.at[phase, n_ctx],
            fresh_send.at[h, 0],
            log_recv.at[phase],
        )
        send(
            "ctx",
            me,
            fresh_to[h],
            fresh_out.at[h],
            part_in.at[phase, n_ctx],
            fresh_send.at[h, 1],
            part_recv.at[phase],
        )
    for p in range(2):
        for i in range(n_ctx + 1, log_in.shape[1]):
            log_in[p, i] = jnp.full((1, HD), NEG, F32)
    arrived(kv, kv_sem)

    for i, (first, last) in enumerate(groups):
        arrived(q_all.at[pl.ds(0, last - first)], q_recv.at[i])
        results = softmax_parts(
            [q_all[b] for b in range(first, last)],
            [keys_of(b) for b in range(first, last)],
            [values_of(b) for b in range(first, last)],
            [selected_of(b) for b in range(first, last)],
        )
        for b, (normed, log) in zip(range(first, last), results):
            for h in range(2):
                part_out[2 * b + h] = normed[h * span : (h + 1) * span]
                log_out[2 * b + h] = as_row(log[h * span : (h + 1) * span])
        for u in range(2 * first, 2 * last):
            to, p = joiner_of(u % n_ctx, n_ctx), u // n_ctx
            send("ctx", me, to, log_out.at[u], log_in.at[p, me], log_send, log_recv.at[p])
            send("ctx", me, to, part_out.at[u], part_in.at[p, me], part_send, part_recv.at[p])

    for p in range(2):
        arrived(log_in.at[p, pl.ds(0, n_ctx + 1)], log_recv.at[p])
        logs = log_in[p].reshape(log_in.shape[1], HD)
        shares = jnp.exp2(logs - jnp.max(logs, axis=0, keepdims=True))
        columns = jnp.transpose(shares)[0:span]
        inverse = 1.0 / jnp.sum(columns, axis=1, keepdims=True)
        arrived(part_in.at[p], part_recv.at[p])
        chains = [jnp.zeros((span, HD), F32) for _ in range(4)]
        for i in range(n_ctx + 1):
            chains[i % 4] += part_in[p, i].astype(F32) * columns[:, i : i + 1]
        joined = (chains[0] + chains[1]) + (chains[2] + chains[3])
        att_own[p] = (joined * inverse).astype(BF16)
        place = half + p * n_ctx
        att_sem = att_recv.at[group_of(place >> 1)]
        for d in others_list:
            remote("ctx", owner(d), att_own.at[p], att_all.at[place], att_send, att_sem).start()
        pltpu.make_async_copy(att_own.at[p], att_all.at[place], att_sem).start()

    w_copy.wait()
    for i, (first, last) in enumerate(groups):
        units = pl.ds(2 * first, 2 * (last - first))
        arrived(att_all.at[units], att_recv.at[i])
        base, count = first * rows, (last - first) * steps
        att32[base : base + count * GROUPS, :] = (
            att_all[2 * first : 2 * last].astype(F32).reshape(count * GROUPS, HD)
        )
        flat = jnp.concatenate(
            [att32[pl.ds(base + g, count, stride=GROUPS), :].astype(BF16) for g in range(GROUPS)],
            axis=1,
        )
        mixed = jnp.dot(flat, w[...], preferred_element_type=F32).astype(BF16)
        for to in range(first // block, last // block):
            row = (to * block - first) * steps
            mix_out[to] = mixed[row : row + block * steps]
        for to in range(first // block, last // block):
            send("head", my_head, to, mix_out.at[to], mix_in.at[my_head], mix_send, mix_recv)

    arrived(q_all.at[pl.ds(0, n_ctx - 1)], q_send)
    arrived(part_out.at[pl.ds(0, 2 * n_ctx - 2)], part_send)
    arrived(log_out.at[pl.ds(0, 2 * n_ctx - 2)], log_send)
    arrived(att_all.at[pl.ds(0, 2 * n_ctx - 2)], att_send)
    for h in range(2):

        @pl.when(me != fresh_to[h])
        def _():
            arrived(fresh_log.at[h], fresh_send.at[h, 0])
            arrived(fresh_out.at[h], fresh_send.at[h, 1])

    arrived(mix_out.at[pl.ds(0, n_head - 1)], mix_send)
    arrived(mix_in, mix_recv)
    total = jnp.sum(mix_in[...].astype(F32), axis=0)
    for i in range(out_ref.shape[0]):
        out_ref[i] = total[i * steps : (i + 1) * steps].astype(BF16)


def local(queries, kv_cache, new_kv, selected, out_weight, *, n_ctx, n_head):
    steps, _, width = queries.shape
    batch, pages = kv_cache.shape[:2]
    rows = steps * GROUPS
    columns = out_weight.shape[1]
    own = batch // n_head * steps
    dma = pltpu.SemaphoreType.DMA
    any_space = pl.BlockSpec(memory_space=pl.ANY)
    sel = jnp.transpose(selected, (0, 3, 2, 1))
    result = pl.pallas_call(
        functools.partial(kernel, n_ctx=n_ctx, n_head=n_head),
        out_shape=pltpu.VMEM((own // steps, steps, columns), BF16),
        in_specs=[any_space] * 5,
        out_specs=pl.BlockSpec(memory_space=pltpu.VMEM),
        scratch_shapes=[
            pltpu.VMEM((steps, width), BF16),
            pltpu.VMEM((steps, 2, HD), BF16),
            pltpu.VMEM(sel.shape, jnp.int32),
            pltpu.VMEM(kv_cache.shape, BF16),
            pltpu.VMEM(out_weight.shape, BF16),
            pltpu.VMEM((rows, HD), F32),
            pltpu.VMEM((rows, HD), BF16),
            pltpu.VMEM((batch, rows, HD), BF16),
            pltpu.VMEM((batch, rows, pages * PAGE), F32),
            pltpu.VMEM((2, rows // 2, HD), BF16),
            pltpu.VMEM((2, 1, HD), F32),
            pltpu.VMEM((2 * batch, rows // 2, HD), BF16),
            pltpu.VMEM((2, n_ctx + 1, rows // 2, HD), BF16),
            pltpu.VMEM((2 * batch, 1, HD), F32),
            pltpu.VMEM((2, n_ctx + 8, 1, HD), F32),
            pltpu.VMEM((2, rows // 2, HD), BF16),
            pltpu.VMEM((2 * batch, rows // 2, HD), BF16),
            pltpu.VMEM((batch * rows, HD), F32),
            pltpu.VMEM((n_head, own, columns), BF16),
            pltpu.VMEM((n_head, own, columns), BF16),
            dma((3,)),
            dma,
            dma,
            dma,
            dma((4,)),
            dma,
            dma((2,)),
            dma,
            dma((2,)),
            dma((2, 2)),
            dma,
            dma((4,)),
            dma,
            dma,
        ],
        compiler_params=pltpu.CompilerParams(
            collective_id=0, has_side_effects=True, vmem_limit_bytes=56 * 1024 * 1024
        ),
    )(
        queries.reshape(steps, width),
        kv_cache,
        new_kv.reshape(steps, 2, HD),
        sel,
        out_weight,
    )
    return result


def solution(mesh):
    n_ctx, n_head = mesh.shape["ctx"], mesh.shape["head"]
    return jax.shard_map(
        functools.partial(local, n_ctx=n_ctx, n_head=n_head),
        mesh=mesh,
        in_specs=(
            P(None, "ctx", "head"),
            P(None, "ctx", None, None, "head"),
            P(None, "ctx", None, "head"),
            P(None, None, "head", None),
            P("head", "ctx"),
        ),
        out_specs=P("head", None, "ctx"),
        check_vma=False,
    )
```

```python
import functools
import math

import jax
import jax.numpy as jnp
from jax import lax
from jax.experimental import pallas as pl
from jax.experimental.pallas import tpu as pltpu
from jax.sharding import PartitionSpec as P

HQ = 64
KVH = 8
HD = 128
PAGE = 64
GROUPS = HQ // KVH

NEG = -1e30
EXPONENT = HD ** (-0.5) * math.log2(math.e)
BF16 = jnp.bfloat16
F32 = jnp.float32
MESH = pl.DeviceIdType.MESH


def axes_of(size):
    return {32: (4, 4, 2), 8: (2, 2, 2)}[size]


def displacements(size):
    nx, ny, nc = axes_of(size)
    every = [(x, y, c) for x in range(nx) for y in range(ny) for c in range(nc)][1:]
    return sorted(every, key=lambda d: -min(d[0], nx - d[0]) - min(d[1], ny - d[1]))


def half_of(x, y, c, size):
    nx, ny, _ = axes_of(size)
    return c * (nx * ny) + x * ny + y


def log2_of(size):
    return size.bit_length() - 1


def joiner_of(half, size):
    nx, ny, nc = axes_of(size)
    c, place = half >> log2_of(nx * ny), half & (nx * ny - 1)
    x, y = place >> log2_of(ny), place & (ny - 1)
    return (x * ny + y) * nc + c


def by_distance(size):
    return sorted(range(1, size), key=lambda d: -min(d, size - d))


def softmax_parts(queries, keys, values, masked):
    scores = [
        mask(lax.dot_general(q, k, (((1,), (1,)), ((), ())), preferred_element_type=F32))
        for q, k, mask in zip(queries, keys, masked)
    ]
    tops = [jnp.max(x, axis=-1, keepdims=True) for x in scores]
    expos = [jnp.exp2((x - top) * EXPONENT) for x, top in zip(scores, tops)]
    totals = [jnp.sum(x, axis=-1, keepdims=True) for x in expos]
    sums = [
        jnp.dot(x.astype(BF16), v, preferred_element_type=F32) for x, v in zip(expos, values)
    ]
    return [
        ((x * (1.0 / total)).astype(BF16), top * EXPONENT + jnp.log2(total))
        for x, top, total in zip(sums, tops, totals)
    ]


def as_row(column):
    lane = lax.broadcasted_iota(jnp.int32, (8, HD), 1)
    sublane = lax.broadcasted_iota(jnp.int32, (8, HD), 0)
    spread = jnp.zeros((8, HD), F32)
    for v in range(column.shape[0] // 8):
        spread = jnp.where(lane == sublane + 8 * v, column[8 * v : 8 * v + 8], spread)
    return jnp.sum(spread, axis=0, keepdims=True)


def kernel(
    q_hbm,
    kv_hbm,
    new_hbm,
    sel_hbm,
    w_hbm,
    out_ref,
    q_in,
    new_in,
    sel_in,
    kv,
    w,
    rows32,
    q_own,
    q_all,
    bias,
    fresh_out,
    fresh_log,
    part_out,
    part_in,
    log_out,
    log_in,
    att_own,
    att_all,
    att32,
    mix_out,
    mix_in,
    small_sem,
    kv_sem,
    w_sem,
    q_send,
    q_recv,
    part_send,
    part_recv,
    log_send,
    log_recv,
    fresh_send,
    att_send,
    att_recv,
    mix_send,
    mix_recv,
    *,
    n_ctx,
    n_head,
):
    steps = q_in.shape[0]
    pages = kv.shape[1]
    tokens = pages * PAGE
    rows = steps * GROUPS
    me = lax.axis_index("ctx")
    my_head = lax.axis_index("head")

    nx, ny, nc = axes_of(n_ctx)
    others_list = displacements(n_ctx)
    x, y, c = me // (ny * nc), (me // nc) & (ny - 1), me & (nc - 1)
    half = half_of(x, y, c, n_ctx)
    block = n_ctx // n_head
    bounds = sorted({0, block, 2 * block, n_ctx // 2, n_ctx})
    groups = list(zip(bounds, bounds[1:]))
    starts = [group[0] for group in groups]

    def owner(d):
        return (((x + d[0]) & (nx - 1)) * ny + ((y + d[1]) & (ny - 1))) * nc + ((c + d[2]) & (nc - 1))

    def group_of(sequence):
        return sum((sequence >= start).astype(jnp.int32) for start in starts[1:])

    def send(axis, here, to, src, dst, send_sem, recv_sem):
        @pl.when(here == to)
        def _():
            pltpu.make_async_copy(src, dst, recv_sem).start()

        @pl.when(here != to)
        def _():
            remote(axis, to, src, dst, send_sem, recv_sem).start()

    def remote(axis, to, src, dst, send_sem, recv_sem):
        return pltpu.make_async_remote_copy(
            src_ref=src,
            dst_ref=dst,
            send_sem=send_sem,
            recv_sem=recv_sem,
            device_id={axis: to},
            device_id_type=MESH,
        )

    def arrived(ref, sem):
        pltpu.make_async_copy(ref, ref, sem).wait()

    q_copy = pltpu.make_async_copy(q_hbm, q_in, small_sem.at[0])
    sel_copy = pltpu.make_async_copy(sel_hbm, sel_in, small_sem.at[1])
    new_copy = pltpu.make_async_copy(new_hbm, new_in, small_sem.at[2])
    w_copy = pltpu.make_async_copy(w_hbm, w, w_sem)
    q_copy.start()
    sel_copy.start()
    new_copy.start()

    barrier = pltpu.get_barrier_semaphore()

    for d in others_list:
        pl.semaphore_signal(barrier, inc=1, device_id={"ctx": owner(d)}, device_id_type=MESH)
    for d in by_distance(n_head):
        to = lax.rem(my_head + d, n_head)
        pl.semaphore_signal(barrier, inc=1, device_id={"head": to}, device_id_type=MESH)

    chunk = kv.shape[0] // 4
    for i in range(4):
        part = pl.ds(i * chunk, chunk)
        pltpu.make_async_copy(kv_hbm.at[part], kv.at[part], kv_sem).start()
    w_copy.start()

    q_copy.wait()
    for s in range(steps):
        for g in range(GROUPS):
            rows32[s * GROUPS + g : s * GROUPS + g + 1, :] = q_in[
                s : s + 1, g * HD : (g + 1) * HD
            ].astype(F32)
    q_own[...] = rows32[...].astype(BF16)

    pl.semaphore_wait(barrier, n_ctx - 1 + n_head - 1)

    q_sem = q_recv.at[group_of(me)]
    for d in others_list:
        remote("ctx", owner(d), q_own, q_all.at[me], q_send, q_sem).start()
    pltpu.make_async_copy(q_own, q_all.at[me], q_sem).start()

    sel_copy.wait()
    number = lax.broadcasted_iota(jnp.int32, (pages, n_ctx), 0) + me * pages
    from_b = lax.broadcasted_iota(jnp.int32, (n_ctx, n_ctx * rows), 0)
    to_lane = lax.broadcasted_iota(jnp.int32, (n_ctx, n_ctx * rows), 1)
    chosen = jnp.zeros((pages, n_ctx * rows), F32)
    for s in range(steps):
        hit = jnp.zeros((pages, n_ctx), F32)
        for j in range(sel_in.shape[1]):
            hit = jnp.where(sel_in[s, j] == number, 1.0, hit)
        spread = jnp.where(((to_lane >> log2_of(rows)) == from_b) & (((to_lane & (rows - 1)) >> 3) == s), 1.0, 0.0)
        chosen += jnp.dot(hit.astype(BF16), spread.astype(BF16), preferred_element_type=F32)
    page = lax.broadcasted_iota(jnp.int32, (pages, tokens), 0)
    token = lax.broadcasted_iota(jnp.int32, (pages, tokens), 1)
    expand = jnp.where((token >> 6) == page, 1.0, 0.0).astype(BF16)
    count = lax.dot_general(
        chosen.astype(BF16), expand, (((0,), (0,)), ((), ())), preferred_element_type=F32
    )
    bias[...] = ((count - 1.0) * -NEG).reshape(bias.shape)

    new_copy.wait()
    new_keys = jnp.concatenate(
        [new_in[:, 0].astype(F32), jnp.zeros((HD - steps, HD), F32)], axis=0
    ).astype(BF16)
    new_values = jnp.concatenate(
        [new_in[:, 1].astype(F32), jnp.zeros((HD - steps, HD), F32)], axis=0
    ).astype(BF16)
    step_of = lax.broadcasted_iota(jnp.int32, (rows, HD), 0) >> 3
    place = lax.broadcasted_iota(jnp.int32, (rows, HD), 1)

    def causal(scores):
        return jnp.where(place <= step_of, scores, NEG)

    def selected_of(b):
        def mask(scores):
            return scores + bias[b]

        return mask

    def keys_of(b):
        return kv[b, :, 0].reshape(tokens, HD)

    def values_of(b):
        return kv[b, :, 1].reshape(tokens, HD)

    own = q_own[...]
    ((normed, log),) = softmax_parts([own], [new_keys], [new_values], [causal])
    span = rows // 2
    phase = me >> log2_of(n_ctx // 2)
    fresh_to = [joiner_of((2 * me + h) & (n_ctx - 1), n_ctx) for h in range(2)]
    for h in range(2):
        fresh_out[h] = normed[h * span : (h + 1) * span]
        fresh_log[h] = as_row(log[h * span : (h + 1) * span])
    for h in range(2):
        send(
            "ctx",
            me,
            fresh_to[h],
            fresh_log.at[h],
            log_in.at[phase, n_ctx],
            fresh_send.at[h, 0],
            log_recv.at[phase],
        )
        send(
            "ctx",
            me,
            fresh_to[h],
            fresh_out.at[h],
            part_in.at[phase, n_ctx],
            fresh_send.at[h, 1],
            part_recv.at[phase],
        )
    for p in range(2):
        for i in range(n_ctx + 1, log_in.shape[1]):
            log_in[p, i] = jnp.full((1, HD), NEG, F32)
    arrived(kv, kv_sem)

    for i, (first, last) in enumerate(groups):
        arrived(q_all.at[pl.ds(0, last - first)], q_recv.at[i])
        results = softmax_parts(
            [q_all[b] for b in range(first, last)],
            [keys_of(b) for b in range(first, last)],
            [values_of(b) for b in range(first, last)],
            [selected_of(b) for b in range(first, last)],
        )
        for b, (normed, log) in zip(range(first, last), results):
            for h in range(2):
                part_out[2 * b + h] = normed[h * span : (h + 1) * span]
                log_out[2 * b + h] = as_row(log[h * span : (h + 1) * span])
        for u in range(2 * first, 2 * last):
            to, p = joiner_of(u % n_ctx, n_ctx), u // n_ctx
            send("ctx", me, to, log_out.at[u], log_in.at[p, me], log_send, log_recv.at[p])
            send("ctx", me, to, part_out.at[u], part_in.at[p, me], part_send, part_recv.at[p])

    for p in range(2):
        arrived(log_in.at[p, pl.ds(0, n_ctx + 1)], log_recv.at[p])
        logs = log_in[p].reshape(log_in.shape[1], HD)
        shares = jnp.exp2(logs - jnp.max(logs, axis=0, keepdims=True))
        columns = jnp.transpose(shares)[0:span]
        inverse = 1.0 / jnp.sum(columns, axis=1, keepdims=True)
        arrived(part_in.at[p], part_recv.at[p])
        chains = [jnp.zeros((span, HD), F32) for _ in range(4)]
        for i in range(n_ctx + 1):
            chains[i % 4] += part_in[p, i].astype(F32) * columns[:, i : i + 1]
        joined = (chains[0] + chains[1]) + (chains[2] + chains[3])
        att_own[p] = (joined * inverse).astype(BF16)
        place = half + p * n_ctx
        att_sem = att_recv.at[group_of(place >> 1)]
        for d in others_list:
            remote("ctx", owner(d), att_own.at[p], att_all.at[place], att_send, att_sem).start()
        pltpu.make_async_copy(att_own.at[p], att_all.at[place], att_sem).start()

    w_copy.wait()
    for i, (first, last) in enumerate(groups):
        units = pl.ds(2 * first, 2 * (last - first))
        arrived(att_all.at[units], att_recv.at[i])
        base, count = first * rows, (last - first) * steps
        att32[base : base + count * GROUPS, :] = (
            att_all[2 * first : 2 * last].astype(F32).reshape(count * GROUPS, HD)
        )
        flat = jnp.concatenate(
            [att32[pl.ds(base + g, count, stride=GROUPS), :].astype(BF16) for g in range(GROUPS)],
            axis=1,
        )
        mixed = jnp.dot(flat, w[...], preferred_element_type=F32).astype(BF16)
        for to in range(first // block, last // block):
            row = (to * block - first) * steps
            mix_out[to] = mixed[row : row + block * steps]
        for to in range(first // block, last // block):
            send("head", my_head, to, mix_out.at[to], mix_in.at[my_head], mix_send, mix_recv)

    arrived(q_all.at[pl.ds(0, n_ctx - 1)], q_send)
    arrived(part_out.at[pl.ds(0, 2 * n_ctx - 2)], part_send)
    arrived(log_out.at[pl.ds(0, 2 * n_ctx - 2)], log_send)
    arrived(att_all.at[pl.ds(0, 2 * n_ctx - 2)], att_send)
    for h in range(2):

        @pl.when(me != fresh_to[h])
        def _():
            arrived(fresh_log.at[h], fresh_send.at[h, 0])
            arrived(fresh_out.at[h], fresh_send.at[h, 1])

    arrived(mix_out.at[pl.ds(0, n_head - 1)], mix_send)
    arrived(mix_in, mix_recv)
    total = jnp.sum(mix_in[...].astype(F32), axis=0)
    for i in range(out_ref.shape[0]):
        out_ref[i] = total[i * steps : (i + 1) * steps].astype(BF16)


def local(queries, kv_cache, new_kv, selected, out_weight, *, n_ctx, n_head):
    steps, _, width = queries.shape
    batch, pages = kv_cache.shape[:2]
    rows = steps * GROUPS
    columns = out_weight.shape[1]
    own = batch // n_head * steps
    dma = pltpu.SemaphoreType.DMA
    any_space = pl.BlockSpec(memory_space=pl.ANY)
    sel = jnp.transpose(selected, (0, 3, 2, 1))
    result = pl.pallas_call(
        functools.partial(kernel, n_ctx=n_ctx, n_head=n_head),
        out_shape=pltpu.VMEM((own // steps, steps, columns), BF16),
        in_specs=[any_space] * 5,
        out_specs=pl.BlockSpec(memory_space=pltpu.VMEM),
        scratch_shapes=[
            pltpu.VMEM((steps, width), BF16),
            pltpu.VMEM((steps, 2, HD), BF16),
            pltpu.VMEM(sel.shape, jnp.int32),
            pltpu.VMEM(kv_cache.shape, BF16),
            pltpu.VMEM(out_weight.shape, BF16),
            pltpu.VMEM((rows, HD), F32),
            pltpu.VMEM((rows, HD), BF16),
            pltpu.VMEM((batch, rows, HD), BF16),
            pltpu.VMEM((batch, rows, pages * PAGE), F32),
            pltpu.VMEM((2, rows // 2, HD), BF16),
            pltpu.VMEM((2, 1, HD), F32),
            pltpu.VMEM((2 * batch, rows // 2, HD), BF16),
            pltpu.VMEM((2, n_ctx + 1, rows // 2, HD), BF16),
            pltpu.VMEM((2 * batch, 1, HD), F32),
            pltpu.VMEM((2, n_ctx + 8, 1, HD), F32),
            pltpu.VMEM((2, rows // 2, HD), BF16),
            pltpu.VMEM((2 * batch, rows // 2, HD), BF16),
            pltpu.VMEM((batch * rows, HD), F32),
            pltpu.VMEM((n_head, own, columns), BF16),
            pltpu.VMEM((n_head, own, columns), BF16),
            dma((3,)),
            dma,
            dma,
            dma,
            dma((4,)),
            dma,
            dma((2,)),
            dma,
            dma((2,)),
            dma((2, 2)),
            dma,
            dma((4,)),
            dma,
            dma,
        ],
        compiler_params=pltpu.CompilerParams(
            collective_id=0, has_side_effects=True, vmem_limit_bytes=56 * 1024 * 1024
        ),
    )(
        queries.reshape(steps, width),
        kv_cache,
        new_kv.reshape(steps, 2, HD),
        sel,
        out_weight,
    )
    return result


def solution(mesh):
    n_ctx, n_head = mesh.shape["ctx"], mesh.shape["head"]
    return jax.shard_map(
        functools.partial(local, n_ctx=n_ctx, n_head=n_head),
        mesh=mesh,
        in_specs=(
            P(None, "ctx", "head"),
            P(None, "ctx", None, None, "head"),
            P(None, "ctx", None, "head"),
            P(None, None, "head", None),
            P("head", "ctx"),
        ),
        out_specs=P("head", None, "ctx"),
        check_vma=False,
    )
```
